32 devices in a mesh: dp: 2 (over core), tensor: 16 (over z, y, x).
Axes of the slice: x: 2, y: 2, z: 4, core: 2. Of those that a mesh axis runs over, the one named last changes fastest.
Arguments:
- gate_pre: bfloat16 [1024, 16384], P('dp', 'tensor'), may hold values from -6 to 6
- up_pre: bfloat16 [1024, 16384], P('dp', 'tensor'), may hold values from -6 to 6
- down_weight: bfloat16 [16384, 4096], P('tensor'), may hold values from -0.0625 to 0.0625
- block_mask: int32 [128, 32], P('tensor'), may hold values from 0 to 1, as said below
- out_grad: bfloat16 [1024, 4096], P(('dp', 'tensor')), may hold values from -6 to 6
Outputs:
- layer_out: bfloat16 [1024, 4096], P(('dp', 'tensor'))
- gate_grad: bfloat16 [1024, 16384], P('dp', 'tensor')
- up_grad: bfloat16 [1024, 16384], P('dp', 'tensor')
- weight_grad: bfloat16 [16384, 4096], P('tensor')
The draws below stay inside these ranges and needn't reach their ends.
Inputs may be any that keep to these rules, and one draw needn't show every extreme that they name: `block_mask`: each tensor shard's 8 x 32 blocks hold between 64 and 192 kept blocks; in every draw some shard keeps exactly 192.
All inputs are finite; a program needn't handle non-finite values.
Results may differ from the reference program's by a relative error of at most 0.0049.
Values may be sent and summed in bfloat16 or wider, within the bound.
A program may use at most 128 MiB of HBM per device.

```python
import math
import jax
import jax.numpy as jnp

D = 4096
FF = 16384
TOKENS = 1024
SHARDS = 16
NB_F = 128
NB_D = 32
BLOCKS_SHARD = 256
KEEP_MAX = 192
KEEP_LO = 64


def draw_block_mask(key, part):
    shard_keys = jax.random.split(jax.random.fold_in(key, 11), SHARDS)

    def shard_ranks(single):
        return jax.random.permutation(single, BLOCKS_SHARD)
    ranks = jax.vmap(shard_ranks)(shard_keys)
    counts = jax.random.randint(jax.random.fold_in(key, 12), (SHARDS,), KEEP_LO, KEEP_MAX + 1)
    busiest = jax.random.randint(jax.random.fold_in(key, 13), (), 0, SHARDS)
    counts = jnp.where(jnp.arange(SHARDS) == busiest, KEEP_MAX, counts)
    flags = (ranks < counts[:, None]).astype(jnp.int32)
    return flags.reshape(NB_F, NB_D)


def block_scale(key, dims, pieces, low, top_value):
    factor_of = 1.0
    for axis_at, shards_of in pieces:
        heights = jax.random.uniform(jax.random.fold_in(jax.random.fold_in(key, 6), axis_at), (shards_of,), jnp.float32, low / len(pieces), top_value / len(pieces))
        factor_of = factor_of * jnp.repeat(jnp.exp(heights), dims[axis_at] // shards_of).reshape((-1,) + (1,) * (len(dims) - 1 - axis_at))
    return factor_of


def bell_draw(stream_key, shape, spread, reach, cuts=(), kind=jnp.bfloat16):
    gain = block_scale(stream_key, shape, cuts, -0.22, 0.18) if cuts else 1.0
    values = jax.random.normal(stream_key, shape, jnp.float32) * spread * gain
    return jnp.minimum(jnp.maximum(values, -reach), reach).astype(kind)


def setup_inputs(seed: int = 0) -> dict:
    arg_keys = jax.random.split(jax.random.key(seed), 6)
    gate_pre = bell_draw(arg_keys[0], (TOKENS, FF), 1.0, 6.0, ((0, 2), (1, 16)))
    up_pre = bell_draw(arg_keys[1], (TOKENS, FF), 1.0, 6.0, ((0, 2), (1, 16)))
    down_weight = bell_draw(arg_keys[2], (FF, D), (FF // 2) ** -0.5, 0.0625, ((0, 16),))
    block_mask = draw_block_mask(jax.random.fold_in(arg_keys[5], 71), 0)
    out_grad = bell_draw(arg_keys[4], (TOKENS, D), 1.0, 6.0, ((0, 32),))
    return {"gate_pre": gate_pre, "up_pre": up_pre, "down_weight": down_weight, "block_mask": block_mask, "out_grad": out_grad}


def expand_mask(matrix, mask):
    nbf, nbd = mask.shape
    blocks = matrix.reshape(nbf, 128, nbd, 128) * mask.astype(matrix.dtype)[:, None, :, None]
    return blocks.reshape(nbf * 128, nbd * 128)

def reference(gate_pre, up_pre, down_weight, block_mask, out_grad):
    masked = expand_mask(down_weight, block_mask)
    gate_val = gate_pre.astype(jnp.float32)
    up_val = up_pre.astype(jnp.float32)
    sigmoid_gate = jax.nn.sigmoid(gate_val)
    silu_gate = gate_val * sigmoid_gate
    hidden = (silu_gate * up_val).astype(jnp.bfloat16)
    layer_out = jnp.dot(hidden, masked, preferred_element_type=jnp.float32).astype(jnp.bfloat16)
    hidden_grad = jnp.dot(out_grad, masked.T, preferred_element_type=jnp.float32)
    gate_grad = (hidden_grad * up_val * sigmoid_gate * (1.0 + gate_val * (1.0 - sigmoid_gate))).astype(jnp.bfloat16)
    up_grad = (hidden_grad * silu_gate).astype(jnp.bfloat16)
    grad_scale = 1.0 / math.sqrt(TOKENS)
    total = jnp.dot(hidden.T, out_grad, preferred_element_type=jnp.float32) * grad_scale
    weight_grad = expand_mask(total, block_mask.astype(jnp.float32)).astype(jnp.bfloat16)
    return (layer_out, gate_grad, up_grad, weight_grad)
```

```python
import functools
import math

import jax
import jax.numpy as jnp
from jax import lax
from jax.experimental import pallas as pl
from jax.experimental.pallas import tpu as pltpu
from jax.sharding import PartitionSpec as P

BLOCK = 128
ORDER = (0, 1, 3, 2)
REST = 8


def remote(src, dst, sends, recvs, at, device):
    return pltpu.make_async_remote_copy(
        src_ref=src,
        dst_ref=dst,
        send_sem=sends.at[at],
        recv_sem=recvs.at[at],
        device_id=device,
        device_id_type=pl.DeviceIdType.MESH,
    )


def fused_kernel(
    scale,
    gate_hbm, up_hbm, weight_hbm, mask_ref, grad_hbm,
    final, gate_grad, up_grad, weight_grad,
    gate, up, weight, cot, hidden, hidden_t, partial,
    first, second, third, send_second, send_third,
    rest_third, rest_second, rest_first, send_rest_second, send_rest_first,
    in_sem,
    z_send, z_recv, hop1_send, hop1_recv, hop2_send, hop2_recv, core_send, core_recv,
    sum1_send, sum1_recv, sum2_send, sum2_recv, sum3_send, sum3_recv,
    rest_send, rest_recv, back_send, back_recv,
):
    d = lax.axis_index("dp")
    t = lax.axis_index("tensor")
    x = t % 2
    y = (t // 2) % 2
    z = t // 4
    ff, width = weight.shape
    tokens = gate.shape[0]
    rest = width // REST
    half = (width - rest) // 2
    halves = (pl.ds(0, half), pl.ds(half, half))
    both, last = pl.ds(0, 2 * half), pl.ds(2 * half, rest)
    zs = [z] + [(z + k) % 4 for k in (1, 2, 3)]
    x_peer = {"tensor": z * 4 + y * 2 + (1 - x)}
    y_peer = {"tensor": z * 4 + (1 - y) * 2 + x}
    core_peer = {"dp": 1 - d}
    z_peer = [None] + [{"tensor": zs[k] * 4 + y * 2 + x} for k in (1, 2, 3)]

    loads = [
        pltpu.make_async_copy(gate_hbm, gate, in_sem.at[0]),
        pltpu.make_async_copy(up_hbm, up, in_sem.at[1]),
        pltpu.make_async_copy(weight_hbm.at[:, last], weight.at[:, last], in_sem.at[2]),
        pltpu.make_async_copy(weight_hbm.at[:, both], weight.at[:, both], in_sem.at[3]),
        pltpu.make_async_copy(grad_hbm, cot.at[d, z, y, x], in_sem.at[4]),
    ]
    for copy in loads:
        copy.start()

    barrier = pltpu.get_barrier_semaphore()
    peers = [x_peer, y_peer, core_peer] + z_peer[1:]
    for peer in peers:
        pl.semaphore_signal(barrier, inc=1, device_id=peer, device_id_type=pl.DeviceIdType.MESH)
    pl.semaphore_wait(barrier, len(peers))

    rest_x = remote(
        grad_hbm.at[:, last], cot.at[d, z, y, x, :, last], rest_send, rest_recv, 0, x_peer
    )
    rest_x.start()
    rest_z = {}
    along_z = {}
    for k in (1, 3, 2):
        along_z[k] = remote(
            grad_hbm.at[:, both], cot.at[d, z, y, x, :, both], z_send, z_recv, k - 1, z_peer[k]
        )
        along_z[k].start()
    hop1, hop2, to_core = {}, {}, {}

    def start_hop1(k):
        at = zs[(4 - k) % 4]
        for h, peer in enumerate((x_peer, y_peer)):
            dst = cot.at[d, at, y, x, :, halves[h]]
            src = grad_hbm.at[:, halves[h]] if k == 0 else dst
            hop1[k, h] = remote(src, dst, hop1_send, hop1_recv, 2 * k + h, peer)
            hop1[k, h].start()

    def start_hop2(k):
        at = zs[(4 - k) % 4]
        refs = (cot.at[d, at, y, :, :, halves[0]], cot.at[d, at, :, x, :, halves[1]])
        for h, peer in enumerate((y_peer, x_peer)):
            hop1[k, h].wait_recv()
        for h, peer in enumerate((y_peer, x_peer)):
            hop2[k, h] = remote(refs[h], refs[h], hop2_send, hop2_recv, 2 * k + h, peer)
            hop2[k, h].start()

    def start_core(k):
        at = zs[(4 - k) % 4]
        for h in range(2):
            hop2[k, h].wait_recv()
        if k:
            rest_z[k].wait_recv()
        to_core[k] = remote(cot.at[d, at], cot.at[d, at], core_send, core_recv, k, core_peer)
        to_core[k].start()

    start_hop1(0)

    loads[0].wait()
    loads[1].wait()

    def hidden_step(step, _):
        cols = pl.ds(pl.multiple_of(step * 128, 128), 128)
        g = gate[:, cols].astype(jnp.float32)
        u = up[:, cols].astype(jnp.float32)
        value = g * jax.nn.sigmoid(g) * u
        hidden[:, cols] = value.astype(jnp.bfloat16)
        hidden_t[d, cols, :] = value.T.astype(jnp.bfloat16)
        return 0

    lax.fori_loop(0, ff // 128, hidden_step, 0)
    hidden_core = remote(hidden_t.at[d], hidden_t.at[d], core_send, core_recv, 4, core_peer)
    hidden_core.start()

    def forward(base, size):
        wide = 256

        def step(i, _):
            cols = pl.ds(pl.multiple_of(base + i * wide, BLOCK), wide)
            for b in range(ff // BLOCK):
                rows = pl.ds(b * BLOCK, BLOCK)
                for c in range(wide // BLOCK):
                    at = pl.ds(pl.multiple_of(base + i * wide + c * BLOCK, BLOCK), BLOCK)
                    keep = mask_ref[b, base // BLOCK + i * (wide // BLOCK) + c]
                    keep = jnp.full((BLOCK, BLOCK), keep.astype(jnp.float32)).astype(jnp.bfloat16)
                    weight[rows, at] = weight[rows, at] * keep
            part = jnp.dot(hidden[...], weight[:, cols], preferred_element_type=jnp.float32)
            partial[:, :, :, :, cols] = part.astype(jnp.bfloat16).reshape(
                partial.shape[:4] + (wide,)
            )
            return 0

        lax.fori_loop(0, size // wide, step, 0)

    sum1, sum2, sum3 = {}, {}, {}

    def start_sum1(h):
        for k in (1, 3, 2, 0):
            at = zs[k]
            src = (partial.at[at, :, 1 - x, :, halves[0]], partial.at[at, 1 - y, :, :, halves[1]])[h]
            sum1[k, h] = remote(
                src, first.at[h, k], sum1_send, sum1_recv, 2 * k + h, (x_peer, y_peer)[h]
            )
            sum1[k, h].start()

    back_z = {}

    def rest_sum(row, column):
        total = partial[z, row, column, :, last].astype(jnp.float32)
        for k in (1, 2, 3):
            total = total + rest_third[k - 1, row, column].astype(jnp.float32)
        return total

    loads[4].wait()
    rest_x.wait_recv()
    rest_y = remote(
        cot.at[d, z, y, :, :, last], cot.at[d, z, y, :, :, last], rest_send, rest_recv, 1, y_peer
    )
    rest_y.start()
    loads[2].wait()
    forward(2 * half, rest)
    for k in (1, 3, 2):
        back_z[k] = remote(
            partial.at[zs[k], :, :, :, last], rest_third.at[k - 1], back_send, back_recv, k - 1,
            z_peer[k],
        )
        back_z[k].start()
    loads[3].wait()
    forward(0, half)
    start_sum1(0)
    rest_y.wait_recv()
    for k in (1, 3, 2):
        rest_z[k] = remote(
            cot.at[d, z, :, :, :, last], cot.at[d, z, :, :, :, last], rest_send, rest_recv, k + 1,
            z_peer[k],
        )
        rest_z[k].start()
    for k in (1, 3):
        along_z[k].wait_recv()
        start_hop1(k)
    forward(half, half)
    start_sum1(1)
    along_z[2].wait_recv()
    start_hop1(2)

    def start_sum2(k):
        at = zs[k]
        for h in range(2):
            sum1[k, h].wait_recv()
            other = (1 - y, 1 - x)[h]
            mine = (partial[at, 1 - y, x, :, halves[0]], partial[at, y, 1 - x, :, halves[1]])[h]
            total = mine.astype(jnp.float32) + first[h, k, other].astype(jnp.float32)
            send_second[h, k] = total.astype(jnp.bfloat16)
            sum2[k, h] = remote(
                send_second.at[h, k], second.at[h, k], sum2_send, sum2_recv, 2 * k + h,
                (y_peer, x_peer)[h],
            )
            sum2[k, h].start()

    for k in ORDER:
        start_hop2(k)
    for k in (1, 3, 2):
        start_sum2(k)
    start_sum2(0)
    for k in (1, 2, 3):
        back_z[k].wait_recv()
    for column in range(2):
        send_rest_second[column] = rest_sum(1 - y, column).astype(jnp.bfloat16)
    back_y = remote(send_rest_second, rest_second, back_send, back_recv, 3, y_peer)
    back_y.start()

    def own_total(k, h):
        mine = partial[zs[k], y, x, :, halves[h]].astype(jnp.float32)
        near = first[h, k, (y, x)[h]].astype(jnp.float32)
        return mine + near + second[h, k].astype(jnp.float32)

    def start_sum3(k):
        for h in range(2):
            sum2[k, h].wait_recv()
            send_third[h, k - 1] = own_total(k, h).astype(jnp.bfloat16)
            sum3[k, h] = remote(
                send_third.at[h, k - 1], third.at[h, k - 1], sum3_send, sum3_recv, 2 * k + h - 2,
                z_peer[k],
            )
            sum3[k, h].start()

    start_core(0)
    start_core(1)
    start_core(3)
    start_core(2)
    start_sum3(1)
    start_sum3(3)
    start_sum3(2)
    back_y.wait_recv()
    total = rest_sum(y, 1 - x) + rest_second[1 - x].astype(jnp.float32)
    send_rest_first[...] = total.astype(jnp.bfloat16)
    back_x = remote(send_rest_first, rest_first, back_send, back_recv, 4, x_peer)
    back_x.start()

    def grad_step(i, _):
        wide = 256
        rows = pl.ds(pl.multiple_of(i * wide, wide), wide)
        rows_out = cot[d].reshape(tokens, width)
        back = lax.dot_general(
            rows_out, weight[rows, :], (((1,), (1,)), ((), ())), preferred_element_type=jnp.float32
        )
        g = gate[:, rows].astype(jnp.float32)
        u = up[:, rows].astype(jnp.float32)
        s = jax.nn.sigmoid(g)
        gate_grad[:, rows] = (back * u * s * (1.0 + g * (1.0 - s))).astype(jnp.bfloat16)
        up_grad[:, rows] = (back * (g * s)).astype(jnp.bfloat16)
        return 0

    lax.fori_loop(0, ff // 256, grad_step, 0)
    hidden_core.wait_recv()
    for k in ORDER:
        to_core[k].wait_recv()

    wide = 512

    def weight_step(i, _):
        cols = pl.ds(pl.multiple_of(i * wide, wide), wide)
        total = jnp.zeros((ff, wide), jnp.float32)
        for core in range(2):
            total = total + jnp.dot(
                hidden_t[core],
                cot[core, :, :, :, :, cols].reshape(tokens, wide),
                preferred_element_type=jnp.float32,
            )
        for b in range(ff // BLOCK):
            for c in range(wide // BLOCK):
                keep = mask_ref[b, i * (wide // BLOCK) + c].astype(jnp.float32) * scale
                block = total[b * BLOCK : (b + 1) * BLOCK, c * BLOCK : (c + 1) * BLOCK]
                at = pl.ds(pl.multiple_of(i * wide + c * BLOCK, BLOCK), BLOCK)
                weight_grad[pl.ds(b * BLOCK, BLOCK), at] = (block * keep).astype(jnp.bfloat16)
        return 0

    lax.fori_loop(0, width // wide, weight_step, 0)

    for h in range(2):
        sum2[0, h].wait_recv()
        total = own_total(0, h)
        for k in (1, 2, 3):
            sum3[k, h].wait_recv()
            total = total + third[h, k - 1].astype(jnp.float32)
        final[:, halves[h]] = total.astype(jnp.bfloat16)
    back_x.wait_recv()
    total = rest_sum(y, x) + rest_second[x].astype(jnp.float32) + rest_first[...].astype(jnp.float32)
    final[:, last] = total.astype(jnp.bfloat16)

    for copies in (along_z, hop1, hop2, to_core, sum1, sum2, sum3, rest_z, back_z):
        for copy in copies.values():
            copy.wait_send()
    for copy in (hidden_core, rest_x, rest_y, back_y, back_x):
        copy.wait_send()


def keep_in_hbm(array):
    return pltpu.with_memory_space_constraint(array, pltpu.HBM)


def fused(gate_pre, up_pre, down_weight, block_mask, out_grad):
    tokens, ff = gate_pre.shape
    rows, width = out_grad.shape
    rest = width // REST
    half = (width - rest) // 2
    scale = 1.0 / math.sqrt(tokens * 2)
    hbm = pl.BlockSpec(memory_space=pl.ANY)
    bf16 = jnp.bfloat16
    dma = pltpu.SemaphoreType.DMA
    counts = [3, 8, 8, 5, 8, 8, 6, 5, 5]
    results = pl.pallas_call(
        functools.partial(fused_kernel, scale),
        out_shape=(
            pltpu.VMEM((rows, width), bf16),
            pltpu.VMEM((tokens, ff), bf16),
            pltpu.VMEM((tokens, ff), bf16),
            pltpu.VMEM((ff, width), bf16),
        ),
        in_specs=[hbm, hbm, hbm, pl.BlockSpec(memory_space=pltpu.SMEM), hbm],
        out_specs=(pl.BlockSpec(memory_space=pltpu.VMEM),) * 4,
        scratch_shapes=[
            pltpu.VMEM((tokens, ff), bf16),
            pltpu.VMEM((tokens, ff), bf16),
            pltpu.VMEM((ff, width), bf16),
            pltpu.VMEM((2, 4, 2, 2, rows, width), bf16),
            pltpu.VMEM((tokens, ff), bf16),
            pltpu.VMEM((2, ff, tokens), bf16),
            pltpu.VMEM((4, 2, 2, rows, width), bf16),
            pltpu.VMEM((2, 4, 2, rows, half), bf16),
            pltpu.VMEM((2, 4, rows, half), bf16),
            pltpu.VMEM((2, 3, rows, half), bf16),
            pltpu.VMEM((2, 4, rows, half), bf16),
            pltpu.VMEM((2, 3, rows, half), bf16),
            pltpu.VMEM((3, 2, 2, rows, rest), bf16),
            pltpu.VMEM((2, rows, rest), bf16),
            pltpu.VMEM((rows, rest), bf16),
            pltpu.VMEM((2, rows, rest), bf16),
            pltpu.VMEM((rows, rest), bf16),
            dma((5,)),
        ]
        + [dma((count,)) for count in counts for _ in range(2)],
        compiler_params=pltpu.CompilerParams(
            collective_id=0, has_side_effects=True, vmem_limit_bytes=50 * 2**20
        ),
        cost_estimate=pl.CostEstimate(
            flops=8 * tokens * ff * width, bytes_accessed=40 * 2**20, transcendentals=2 * tokens * ff
        ),
    )(*(keep_in_hbm(a) for a in (gate_pre, up_pre, down_weight)), block_mask, keep_in_hbm(out_grad))
    return hand_on(results)


def hand_on_kernel(arrays, *refs):
    srcs, dsts, store_sem = refs[:arrays], refs[arrays : 2 * arrays], refs[2 * arrays]
    stores = [
        pltpu.make_async_copy(src, dst, store_sem.at[n])
        for n, (src, dst) in enumerate(zip(srcs, dsts))
    ]
    for store in stores:
        store.start()
    for store in stores:
        store.wait()


def hand_on(arrays):
    return pl.pallas_call(
        functools.partial(hand_on_kernel, len(arrays)),
        out_shape=tuple(jax.ShapeDtypeStruct(a.shape, a.dtype) for a in arrays),
        in_specs=[pl.BlockSpec(memory_space=pltpu.VMEM)] * len(arrays),
        out_specs=(pl.BlockSpec(memory_space=pl.ANY),) * len(arrays),
        scratch_shapes=[pltpu.SemaphoreType.DMA((len(arrays),))],
        compiler_params=pltpu.CompilerParams(vmem_limit_bytes=2 * 2**20),
    )(*(pltpu.with_memory_space_constraint(a, pltpu.VMEM) for a in arrays))


def local(gate_pre, up_pre, down_weight, block_mask, out_grad):
    blk_rows, blk_cols = block_mask.shape
    ff_local, width = down_weight.shape
    masked = (
        down_weight.reshape(blk_rows, 128, blk_cols, 128)
        * block_mask.astype(jnp.bfloat16)[:, None, :, None]
    ).reshape(ff_local, width)
    gate_val = gate_pre.astype(jnp.float32)
    up_val = up_pre.astype(jnp.float32)
    sigmoid_gate = jax.nn.sigmoid(gate_val)
    silu_gate = gate_val * sigmoid_gate
    hidden = (silu_gate * up_val).astype(jnp.bfloat16)
    layer_out = lax.psum_scatter(
        jnp.dot(hidden, masked, preferred_element_type=jnp.float32),
        "tensor",
        scatter_dimension=0,
        tiled=True,
    ).astype(jnp.bfloat16)
    cot_rows = lax.all_gather(out_grad, "tensor", axis=0, tiled=True)
    hidden_grad = lax.dot_general(
        cot_rows, masked, (((1,), (1,)), ((), ())), preferred_element_type=jnp.float32
    )
    gate_grad = (
        hidden_grad * up_val * sigmoid_gate * (1.0 + gate_val * (1.0 - sigmoid_gate))
    ).astype(jnp.bfloat16)
    up_grad = (hidden_grad * silu_gate).astype(jnp.bfloat16)
    tokens_all = out_grad.shape[0] * lax.axis_size("tensor") * lax.axis_size("dp")
    grad_scale = 1.0 / math.sqrt(tokens_all)
    partial_grad = (
        lax.dot_general(
            hidden, cot_rows, (((0,), (0,)), ((), ())), preferred_element_type=jnp.float32
        )
        * grad_scale
    )
    blocked = (
        partial_grad.reshape(blk_rows, 128, blk_cols, 128)
        * block_mask.astype(jnp.float32)[:, None, :, None]
    )
    summed = lax.psum(blocked.reshape(ff_local, width), "dp")
    weight_grad = summed.astype(jnp.bfloat16)
    return (layer_out, gate_grad, up_grad, weight_grad)


def solution(mesh):
    grouped = mesh.shape["dp"] == 2 and mesh.shape["tensor"] == 16
    return jax.shard_map(
        fused if grouped else local,
        mesh=mesh,
        in_specs=(
            P("dp", "tensor"),
            P("dp", "tensor"),
            P("tensor", None),
            P("tensor", None),
            P(("dp", "tensor"), None),
        ),
        out_specs=(
            P(("dp", "tensor"), None),
            P("dp", "tensor"),
            P("dp", "tensor"),
            P("tensor", None),
        ),
        check_vma=False,
    )
```

```python
import functools
import math

import jax
import jax.numpy as jnp
from jax import lax
from jax.experimental import pallas as pl
from jax.experimental.pallas import tpu as pltpu
from jax.sharding import PartitionSpec as P

BLOCK = 128
STEP = 512
CHUNKS = (("z", 1), ("z", 2), ("z", 2), ("x", 1), ("x", 1), ("x", 1))
CHUNK_SCRATCH = 5


FORWARD = (0, 1, 5, 4, 3, 2)
PLAN = (
    ("gather", 1), ("hop1", 5, 0), ("hop1", 4, 0), ("hop1", 3, 0), ("gather", 0), ("own",),
    ("hop1", 1, 0), ("hop1", 2, 0), ("hop2", 5, 0), ("hop2", 4, 0), ("loads",), ("hop1", 0, 0),
    ("hop2", 3, 0), ("pass", 1, 0), ("pass", 1, 1), ("gather", 2), ("hop1", 1, 1), ("hop1", 1, 2),
    ("hop2", 1, 0), ("hidden",), ("hop2", 2, 0), ("square", 5, 0), ("core", 5, 0), ("pass", 1, 2),
    ("pass", 0, 0), ("gather", 5), ("fwd", 0, 0), ("sum1", 0, 3), ("pass", 2, 0), ("pass", 0, 1),
    ("hop1", 1, 3), ("hop1", 0, 1), ("fwd", 1, 0), ("square", 4, 0), ("gather", 4),
    ("hop2", 1, 2), ("hop1", 0, 2), ("hop2", 1, 1), ("fwd", 1, 1), ("hop1", 2, 1),
    ("square", 2, 0), ("square", 1, 0), ("square", 3, 0), ("hop2", 1, 3), ("core", 4, 0),
    ("gather", 3), ("sum1", 0, 1), ("pass", 5, 0), ("core", 2, 0), ("fwd", 5, 0), ("fwd", 4, 0),
    ("sum1", 1, 2), ("hop2", 0, 2), ("hop2", 0, 0), ("sum2", 0, 3), ("core", 1, 0),
    ("square", 1, 2), ("core", 1, 2), ("pass", 4, 0), ("core", 3, 0), ("core", 5, 1),
    ("square", 1, 1), ("hop2", 0, 1), ("sum1", 0, 0), ("core", 4, 1), ("pass", 2, 1),
    ("hop1", 2, 2), ("sumz", 5, 3), ("hop2", 2, 1), ("sum1", 0, 2), ("fwd", 3, 0),
    ("square", 1, 3), ("core", 1, 3), ("core", 1, 1), ("hg", 1, 0), ("sum2", 0, 1),
    ("pass", 3, 0), ("sumz", 3, 3), ("fwd", 2, 0), ("sum1", 1, 1), ("square", 0, 2),
    ("core", 3, 1), ("fwd", 2, 1), ("pass", 5, 1), ("sum2", 1, 2), ("sumz", 4, 3), ("pass", 2, 2),
    ("pass", 3, 1), ("core", 0, 2), ("sumz", 5, 2), ("total", 0, 3), ("hop1", 2, 3), ("hg", 1, 1),
    ("sum1", 1, 0), ("hcore",), ("wg", 1, 0), ("hop2", 2, 2), ("core", 3, 2), ("total", 1, 2),
    ("pass", 4, 1), ("sum2", 1, 1), ("hop2", 2, 3), ("sum2", 0, 2), ("core", 5, 2),
    ("sum1", 2, 1), ("sum1", 2, 2), ("sum1", 2, 3), ("core", 4, 2), ("square", 2, 1),
    ("square", 0, 0), ("pass", 5, 2), ("sumz", 3, 2), ("core", 2, 1), ("core", 0, 0),
    ("sum2", 0, 0), ("hg", 5, 0), ("core", 5, 3), ("sum1", 1, 3), ("wg", 1, 1), ("sum2", 1, 0),
    ("sum1", 2, 0), ("sumz", 4, 2), ("sumz", 5, 1), ("square", 2, 2), ("wg", 5, 0),
    ("core", 2, 2), ("total", 0, 1), ("square", 0, 1), ("square", 2, 3), ("core", 2, 3),
    ("hg", 2, 0), ("hg", 2, 1), ("wg", 2, 0), ("pass", 0, 2), ("hop1", 0, 3), ("sumz", 3, 1),
    ("sum2", 2, 2), ("hg", 5, 1), ("core", 0, 1), ("sum2", 2, 3), ("pass", 4, 2), ("sum2", 2, 1),
    ("total", 1, 1), ("hg", 4, 0), ("sum2", 1, 3), ("hg", 4, 1), ("sumz", 4, 1), ("wg", 2, 1),
    ("total", 0, 2), ("hop2", 0, 3), ("pass", 3, 2), ("line", 3), ("line", 5), ("sum1", 5, 0),
    ("sum1", 3, 0), ("total", 2, 3), ("line", 4), ("sum1", 4, 0), ("total", 2, 1),
    ("total", 1, 3), ("sum2", 2, 0), ("total", 2, 2), ("core", 4, 3), ("sumz", 0, 3),
    ("hg", 3, 0), ("core", 3, 3), ("sumz", 2, 3), ("square", 0, 3), ("hg", 0, 0), ("core", 0, 3),
    ("sumz", 1, 3), ("sum2", 4, 0), ("sumz", 0, 2), ("sum2", 3, 0), ("sum2", 5, 0), ("hg", 3, 1),
    ("sumz", 2, 2), ("sumz", 0, 1), ("hg", 0, 1), ("sumz", 1, 2), ("sumz", 2, 1), ("endx", 4),
    ("wg", 4, 0), ("sumz", 1, 1), ("endx", 5), ("wg", 3, 0), ("endx", 3), ("endz", 0),
    ("wg", 0, 0), ("endz", 2), ("endz", 1),
)


def remote(src, dst, send, recv, device):
    return pltpu.make_async_remote_copy(
        src_ref=src,
        dst_ref=dst,
        send_sem=send,
        recv_sem=recv,
        device_id=device,
        device_id_type=pl.DeviceIdType.MESH,
    )


def chunk_columns(width):
    unit = width // 8
    at, spans = 0, []
    for _, units in CHUNKS:
        spans.append((at, units * unit))
        at += units * unit
    return spans


def f32(value):
    return value.astype(jnp.float32)


def fused_kernel(
    scale,
    gate_hbm, up_hbm, weight_hbm, mask_ref, grad_hbm,
    final, gate_grad, up_grad, weight_grad,
    gate, up, weight, cot, hidden, hidden_t, partial, acc,
    in_sem, weight_sem, hidden_send, hidden_recv,
    *scratch,
):
    d = lax.axis_index("dp")
    t = lax.axis_index("tensor")
    x = t % 2
    y = (t // 2) % 2
    z = t // 4
    ff, width = weight.shape
    tokens = gate.shape[0]
    bf16 = jnp.bfloat16
    spans = chunk_columns(width)

    mid = ((z + 1) // 2) % 2
    end = 1 - mid
    is_mid = mid == 1
    inner = mid * (3 - z) + end * (1 + z // 3)
    outer = mid * (z - 1) * 3
    far = end * (3 - z) + mid * (2 - z) * 3
    blocks = (z, inner, end * (3 - inner) + mid * outer, far)

    def along(level):
        return {"tensor": level * 4 + y * 2 + x}

    x_peer = {"tensor": z * 4 + y * 2 + (1 - x)}
    y_peer = {"tensor": z * 4 + (1 - y) * 2 + x}
    core_peer = {"dp": 1 - d}
    inner_peer, outer_peer = along(inner), along(outer)

    loads = [
        pltpu.make_async_copy(gate_hbm, gate, in_sem.at[0]),
        pltpu.make_async_copy(up_hbm, up, in_sem.at[1]),
        pltpu.make_async_copy(grad_hbm, cot.at[d, z, y, x], in_sem.at[2]),
    ]
    weight_loads = {}
    for c, (at, size) in enumerate(spans):
        cols = pl.ds(at, size)
        weight_loads[c] = pltpu.make_async_copy(
            weight_hbm.at[:, cols], weight.at[:, cols], weight_sem.at[c]
        )
    for copy in loads:
        copy.start()
    for c in FORWARD:
        weight_loads[c].start()

    barrier = pltpu.get_barrier_semaphore()
    for peer in (x_peer, y_peer, core_peer, inner_peer):
        pl.semaphore_signal(barrier, inc=1, device_id=peer, device_id_type=pl.DeviceIdType.MESH)

    @pl.when(is_mid)
    def _():
        pl.semaphore_signal(
            barrier, inc=1, device_id=outer_peer, device_id_type=pl.DeviceIdType.MESH
        )

    pl.semaphore_wait(barrier, 4 + mid)

    hidden_core = remote(
        hidden_t.at[d], hidden_t.at[d], hidden_send.at[0], hidden_recv.at[0], core_peer
    )
    sent = []
    sent_mid = []

    def go(copy):
        copy.start()
        sent.append(copy)
        return copy

    class Chunk:
        pass

    def both_halves(chunk):
        return ((0, x_peer, y_peer, chunk.halves[0]), (1, y_peer, x_peer, chunk.halves[1]))

    chunks = []
    for c, (kind, _) in enumerate(CHUNKS):
        chunk = Chunk()
        at, size = spans[c]
        chunk.kind, chunk.at, chunk.size = kind, at, size
        chunk.cols = pl.ds(at, size)
        chunk.halves = (pl.ds(at, size // 2), pl.ds(at + size // 2, size // 2))
        chunk.first, chunk.second, chunk.along, chunk.send, chunk.recv = scratch[
            CHUNK_SCRATCH * c : CHUNK_SCRATCH * (c + 1)
        ]
        chunk.hop1, chunk.hop2, chunk.core, chunk.sum1, chunk.sum2 = {}, {}, {}, {}, {}
        chunks.append(chunk)


    def piece(chunk, b):
        if chunk.kind == "z":
            return cot.at[d, b, y, x, :, chunk.cols]
        return cot.at[d, b, :, :, :, chunk.cols]

    def gather_z(chunk):
        own = piece(chunk, z)
        src = grad_hbm.at[:, chunk.cols] if chunk.kind == "z" else own
        go(remote(src, own, chunk.send.at[36], chunk.recv.at[36 + end], inner_peer))

        @pl.when(is_mid)
        def _():
            remote(src, own, chunk.send.at[37], chunk.recv.at[36], outer_peer).start()

        sent_mid.append(remote(src, own, chunk.send.at[37], chunk.recv.at[36], outer_peer))

    def pass_z(chunk, s):
        block = piece(chunk, blocks[s + 1])
        remote(block, block, chunk.send.at[36], chunk.recv.at[36 + s], inner_peer).wait_recv()
        to, slot = ((outer_peer, 1), (inner_peer, 2), (outer_peer, 2))[s]
        copy = remote(block, block, chunk.send.at[38 + s], chunk.recv.at[36 + slot], to)

        @pl.when(is_mid)
        def _():
            copy.start()

        sent_mid.append(copy)

    def hop1(chunk, k):
        for h, near, _, half in both_halves(chunk):
            dst = cot.at[d, blocks[k], y, x, :, half]
            src = grad_hbm.at[:, half] if k == 0 else dst
            n = 2 * k + h
            chunk.hop1[k, h] = go(remote(src, dst, chunk.send.at[n], chunk.recv.at[n], near))

    def hop2(chunk, k):
        for h in range(2):
            chunk.hop1[k, h].wait_recv()
        for h, _, other, half in both_halves(chunk):
            ref = (cot.at[d, blocks[k], y, :, :, half], cot.at[d, blocks[k], :, x, :, half])[h]
            n = 8 + 2 * k + h
            chunk.hop2[k, h] = go(remote(ref, ref, chunk.send.at[n], chunk.recv.at[n], other))

    def square(chunk, k):
        for h in range(2):
            chunk.hop2[k, h].wait_recv()

    def to_core(chunk, k):
        ref = cot.at[d, blocks[k], :, :, :, chunk.cols]
        chunk.core[k] = go(
            remote(ref, ref, chunk.send.at[16 + k], chunk.recv.at[16 + k], core_peer)
        )

    def sum1(chunk, k):
        for h, near, _, half in both_halves(chunk):
            src = (
                partial.at[blocks[k], :, 1 - x, :, half],
                partial.at[blocks[k], 1 - y, :, :, half],
            )[h]
            n = 20 + 2 * k + h
            chunk.sum1[k, h] = go(
                remote(src, chunk.first.at[h, k], chunk.send.at[n], chunk.recv.at[n], near)
            )

    def sum2(chunk, k):
        for h, _, other, half in both_halves(chunk):
            chunk.sum1[k, h].wait_recv()
            row, column, there = ((1 - y, x, 1 - y), (y, 1 - x, 1 - x))[h]
            total = f32(partial[blocks[k], row, column, :, half]) + f32(chunk.first[h, k, there])
            partial[blocks[k], row, column, :, half] = total.astype(bf16)
            n = 28 + 2 * k + h
            chunk.sum2[k, h] = go(
                remote(
                    partial.at[blocks[k], row, column, :, half], chunk.second.at[h, k],
                    chunk.send.at[n], chunk.recv.at[n], other,
                )
            )

    def own_total(chunk, k, h):
        mine = f32(partial[blocks[k], y, x, :, chunk.halves[h]])
        return mine + f32(chunk.first[h, k, (y, x)[h]]) + f32(chunk.second[h, k])

    def square_total(chunk, k):
        for h in range(2):
            chunk.sum2[k, h].wait_recv()
            partial[blocks[k], y, x, :, chunk.halves[h]] = own_total(chunk, k, h).astype(bf16)

    def term(chunk, k):
        if chunk.kind == "z":
            return partial.at[blocks[k], y, x, :, chunk.cols]
        return partial.at[blocks[k], :, :, :, chunk.cols]

    def arrived(chunk, slot):
        ref = chunk.along.at[slot]
        remote(ref, ref, chunk.send.at[41], chunk.recv.at[41 + slot], inner_peer).wait_recv()

    def add_term(chunk, k, slots):
        if chunk.kind == "z":
            total = f32(partial[blocks[k], y, x, :, chunk.cols])
            for slot in slots:
                total = total + f32(chunk.along[slot])
            partial[blocks[k], y, x, :, chunk.cols] = total.astype(bf16)
            return

        wide = 256

        def step(i, _):
            here = pl.ds(pl.multiple_of(i * wide, wide), wide)
            cols = pl.ds(pl.multiple_of(chunk.at + i * wide, wide), wide)
            total = f32(partial[blocks[k], :, :, :, cols])
            for slot in slots:
                total = total + f32(chunk.along[slot, :, :, :, here])
            partial[blocks[k], :, :, :, cols] = total.astype(bf16)
            return 0

        lax.fori_loop(0, chunk.size // wide, step, 0)

    def sum_z(chunk, k):
        @pl.when(is_mid)
        def _():
            arrived(chunk, k)
            add_term(chunk, k, (k,))

        slot = (None, 4 * mid, end, 2 + end)[k]
        to = along(end * inner + mid * outer) if k == 2 else inner_peer
        ref = term(chunk, k)
        go(remote(ref, chunk.along.at[slot], chunk.send.at[41 + k], chunk.recv.at[41 + slot], to))

    def line_total(chunk):
        arrived(chunk, 0)

        @pl.when(is_mid)
        def _():
            arrived(chunk, 4)
            add_term(chunk, 0, (0, 4))

        @pl.when(end == 1)
        def _():
            add_term(chunk, 0, (0,))

    def finish_z(chunk):
        arrived(chunk, 0)
        size = chunk.size // 2

        @pl.when(is_mid)
        def _():
            arrived(chunk, 4)

        for h in range(2):
            chunk.sum2[0, h].wait_recv()
            here = pl.ds(h * size, size)
            total = own_total(chunk, 0, h) + f32(chunk.along[0, :, here])

            @pl.when(is_mid)
            def _():
                final[:, chunk.halves[h]] = (total + f32(chunk.along[4, :, here])).astype(bf16)

            @pl.when(end == 1)
            def _():
                final[:, chunk.halves[h]] = total.astype(bf16)

    def finish_x(chunk):
        for h in range(2):
            chunk.sum2[0, h].wait_recv()
            final[:, chunk.halves[h]] = own_total(chunk, 0, h).astype(bf16)

    graded = [0, 0]

    def hidden_step(step, _):
        cols = pl.ds(pl.multiple_of(step * 128, 128), 128)
        g = f32(gate[:, cols])
        u = f32(up[:, cols])
        value = g * jax.nn.sigmoid(g) * u
        hidden[:, cols] = value.astype(bf16)
        hidden_t[d, cols, :] = value.T.astype(bf16)
        return 0

    def forward(chunk, i):
        base = chunk.at + i * STEP
        cols = pl.ds(base, STEP)
        for b in range(ff // BLOCK):
            rows = pl.ds(b * BLOCK, BLOCK)
            for c in range(STEP // BLOCK):
                at = pl.ds(base + c * BLOCK, BLOCK)
                keep = mask_ref[b, chunk.at // BLOCK + i * (STEP // BLOCK) + c]
                keep = jnp.full((BLOCK, BLOCK), keep.astype(jnp.float32)).astype(bf16)
                weight[rows, at] = weight[rows, at] * keep
        part = jnp.dot(hidden[...], weight[:, cols], preferred_element_type=jnp.float32)
        partial[:, :, :, :, cols] = part.astype(bf16).reshape(partial.shape[:4] + (STEP,))

    def hidden_grad(chunk, part):
        begin, close = graded[part] == 0, graded[part] == len(CHUNKS) - 1
        graded[part] += 1
        wide = 256

        def step(i, _):
            rows = pl.ds(pl.multiple_of(i * wide, wide), wide)
            back = lax.dot_general(
                cot[d, :, :, :, :, chunk.cols].reshape(tokens, chunk.size),
                weight[rows, chunk.cols],
                (((1,), (1,)), ((), ())),
                preferred_element_type=jnp.float32,
            )
            if not begin:
                back = back + acc[:, rows]
            if not close:
                acc[:, rows] = back
                return 0
            g = f32(gate[:, rows])
            u = f32(up[:, rows])
            s = jax.nn.sigmoid(g)
            gate_grad[:, rows] = (back * u * s * (1.0 + g * (1.0 - s))).astype(bf16)
            up_grad[:, rows] = (back * (g * s)).astype(bf16)
            return 0

        count = ff // wide // 2
        lax.fori_loop(part * count, (part + 1) * count, step, 0)

    def weight_step(chunk, i):
        base = chunk.at + i * STEP
        cols = pl.ds(base, STEP)
        total = jnp.zeros((ff, STEP), jnp.float32)
        for core in range(2):
            total = total + jnp.dot(
                hidden_t[core],
                cot[core, :, :, :, :, cols].reshape(tokens, STEP),
                preferred_element_type=jnp.float32,
            )
        for b in range(ff // BLOCK):
            for c in range(STEP // BLOCK):
                keep = mask_ref[b, chunk.at // BLOCK + i * (STEP // BLOCK) + c]
                keep = keep.astype(jnp.float32) * scale
                block = total[b * BLOCK : (b + 1) * BLOCK, c * BLOCK : (c + 1) * BLOCK]
                at = pl.ds(base + c * BLOCK, BLOCK)
                weight_grad[pl.ds(b * BLOCK, BLOCK), at] = (block * keep).astype(bf16)

    def do_loads():
        loads[0].wait()
        loads[1].wait()

    def do_hidden():
        lax.fori_loop(0, ff // 128, hidden_step, 0)
        hidden_core.start()

    def do_forward(c, i):
        if i == 0:
            weight_loads[c].wait()
        forward(chunks[c], i)

    def do_weight(c, i):
        if i == 0:
            for k in range(4):
                chunks[c].core[k].wait_recv()
        weight_step(chunks[c], i)

    actions = {
        "loads": do_loads,
        "hidden": do_hidden,
        "own": lambda: loads[2].wait(),
        "hcore": lambda: hidden_core.wait_recv(),
        "fwd": do_forward,
        "wg": do_weight,
        "hg": lambda c, part: hidden_grad(chunks[c], part),
        "gather": lambda c: gather_z(chunks[c]),
        "pass": lambda c, k: pass_z(chunks[c], k),
        "hop1": lambda c, k: hop1(chunks[c], k),
        "hop2": lambda c, k: hop2(chunks[c], k),
        "square": lambda c, k: square(chunks[c], k),
        "core": lambda c, k: to_core(chunks[c], k),
        "sum1": lambda c, k: sum1(chunks[c], k),
        "sum2": lambda c, k: sum2(chunks[c], k),
        "total": lambda c, k: square_total(chunks[c], k),
        "sumz": lambda c, k: sum_z(chunks[c], k),
        "line": lambda c: line_total(chunks[c]),
        "endz": lambda c: finish_z(chunks[c]),
        "endx": lambda c: finish_x(chunks[c]),
    }
    for name, *args in PLAN:
        actions[name](*args)

    for copy in sent:
        copy.wait_send()

    @pl.when(is_mid)
    def _():
        for copy in sent_mid:
            copy.wait_send()

    hidden_core.wait_send()


def keep_in_hbm(array):
    return pltpu.with_memory_space_constraint(array, pltpu.HBM)


def chunk_scratch(rows, width):
    dma = pltpu.SemaphoreType.DMA
    bf16 = jnp.bfloat16
    scratch = []
    for (kind, _), (_, size) in zip(CHUNKS, chunk_columns(width)):
        levels = 4 if kind == "z" else 1
        held = (rows,) if kind == "z" else (2, 2, rows)
        scratch += [
            pltpu.VMEM((2, levels, 2, rows, size // 2), bf16),
            pltpu.VMEM((2, levels, rows, size // 2), bf16),
            pltpu.VMEM((5,) + held + (size,), bf16),
            dma((46,)),
            dma((46,)),
        ]
    return scratch


def fused(gate_pre, up_pre, down_weight, block_mask, out_grad):
    tokens, ff = gate_pre.shape
    rows, width = out_grad.shape
    scale = 1.0 / math.sqrt(tokens * 2)
    hbm = pl.BlockSpec(memory_space=pl.ANY)
    bf16 = jnp.bfloat16
    dma = pltpu.SemaphoreType.DMA
    results = pl.pallas_call(
        functools.partial(fused_kernel, scale),
        out_shape=(
            pltpu.VMEM((rows, width), bf16),
            pltpu.VMEM((tokens, ff), bf16),
            pltpu.VMEM((tokens, ff), bf16),
            pltpu.VMEM((ff, width), bf16),
        ),
        in_specs=[hbm, hbm, hbm, pl.BlockSpec(memory_space=pltpu.SMEM), hbm],
        out_specs=(pl.BlockSpec(memory_space=pltpu.VMEM),) * 4,
        scratch_shapes=[
            pltpu.VMEM((tokens, ff), bf16),
            pltpu.VMEM((tokens, ff), bf16),
            pltpu.VMEM((ff, width), bf16),
            pltpu.VMEM((2, 4, 2, 2, rows, width), bf16),
            pltpu.VMEM((tokens, ff), bf16),
            pltpu.VMEM((2, ff, tokens), bf16),
            pltpu.VMEM((4, 2, 2, rows, width), bf16),
            pltpu.VMEM((tokens, ff), jnp.float32),
            dma((3,)),
            dma((len(CHUNKS),)),
            dma((1,)),
            dma((1,)),
        ]
        + chunk_scratch(rows, width),
        compiler_params=pltpu.CompilerParams(
            collective_id=0, has_side_effects=True, vmem_limit_bytes=50 * 2**20
        ),
        cost_estimate=pl.CostEstimate(
            flops=8 * tokens * ff * width, bytes_accessed=40 * 2**20, transcendentals=2 * tokens * ff
        ),
    )(*(keep_in_hbm(a) for a in (gate_pre, up_pre, down_weight)), block_mask, keep_in_hbm(out_grad))
    return hand_on(results)


def hand_on_kernel(arrays, *refs):
    srcs, dsts, store_sem = refs[:arrays], refs[arrays : 2 * arrays], refs[2 * arrays]
    stores = [
        pltpu.make_async_copy(src, dst, store_sem.at[n])
        for n, (src, dst) in enumerate(zip(srcs, dsts))
    ]
    for store in stores:
        store.start()
    for store in stores:
        store.wait()


def hand_on(arrays):
    return pl.pallas_call(
        functools.partial(hand_on_kernel, len(arrays)),
        out_shape=tuple(jax.ShapeDtypeStruct(a.shape, a.dtype) for a in arrays),
        in_specs=[pl.BlockSpec(memory_space=pltpu.VMEM)] * len(arrays),
        out_specs=(pl.BlockSpec(memory_space=pl.ANY),) * len(arrays),
        scratch_shapes=[pltpu.SemaphoreType.DMA((len(arrays),))],
        compiler_params=pltpu.CompilerParams(vmem_limit_bytes=2 * 2**20),
    )(*(pltpu.with_memory_space_constraint(a, pltpu.VMEM) for a in arrays))


def local(gate_pre, up_pre, down_weight, block_mask, out_grad):
    blk_rows, blk_cols = block_mask.shape
    ff_local, width = down_weight.shape
    masked = (
        down_weight.reshape(blk_rows, 128, blk_cols, 128)
        * block_mask.astype(jnp.bfloat16)[:, None, :, None]
    ).reshape(ff_local, width)
    gate_val = gate_pre.astype(jnp.float32)
    up_val = up_pre.astype(jnp.float32)
    sigmoid_gate = jax.nn.sigmoid(gate_val)
    silu_gate = gate_val * sigmoid_gate
    hidden = (silu_gate * up_val).astype(jnp.bfloat16)
    layer_out = lax.psum_scatter(
        jnp.dot(hidden, masked, preferred_element_type=jnp.float32),
        "tensor",
        scatter_dimension=0,
        tiled=True,
    ).astype(jnp.bfloat16)
    cot_rows = lax.all_gather(out_grad, "tensor", axis=0, tiled=True)
    hidden_grad = lax.dot_general(
        cot_rows, masked, (((1,), (1,)), ((), ())), preferred_element_type=jnp.float32
    )
    gate_grad = (
        hidden_grad * up_val * sigmoid_gate * (1.0 + gate_val * (1.0 - sigmoid_gate))
    ).astype(jnp.bfloat16)
    up_grad = (hidden_grad * silu_gate).astype(jnp.bfloat16)
    tokens_all = out_grad.shape[0] * lax.axis_size("tensor") * lax.axis_size("dp")
    grad_scale = 1.0 / math.sqrt(tokens_all)
    partial_grad = (
        lax.dot_general(
            hidden, cot_rows, (((0,), (0,)), ((), ())), preferred_element_type=jnp.float32
        )
        * grad_scale
    )
    blocked = (
        partial_grad.reshape(blk_rows, 128, blk_cols, 128)
        * block_mask.astype(jnp.float32)[:, None, :, None]
    )
    summed = lax.psum(blocked.reshape(ff_local, width), "dp")
    weight_grad = summed.astype(jnp.bfloat16)
    return (layer_out, gate_grad, up_grad, weight_grad)


def solution(mesh):
    grouped = mesh.shape["dp"] == 2 and mesh.shape["tensor"] == 16
    return jax.shard_map(
        fused if grouped else local,
        mesh=mesh,
        in_specs=(
            P("dp", "tensor"),
            P("dp", "tensor"),
            P("tensor", None),
            P("tensor", None),
            P(("dp", "tensor"), None),
        ),
        out_specs=(
            P(("dp", "tensor"), None),
            P("dp", "tensor"),
            P("dp", "tensor"),
            P("tensor", None),
        ),
        check_vma=False,
    )
```

```python
import functools
import math

import jax
import jax.numpy as jnp
from jax import lax
from jax.experimental import pallas as pl
from jax.experimental.pallas import tpu as pltpu
from jax.sharding import PartitionSpec as P

BLOCK = 128
STEP = 512
CHUNKS = (("z", 2), ("z", 1), ("z", 2), ("x", 1), ("x", 1), ("x", 1))
CHUNK_SCRATCH = 5


FORWARD = (0, 1, 2, 3, 4, 5)
PLAN = (
    ("hop1", 4, 0), ("gather", 1), ("gather", 2), ("hop1", 5, 0), ("own",), ("hop1", 3, 0),
    ("hop1", 2, 0), ("hop1", 1, 0), ("hop2", 4, 0), ("gather", 0), ("hop1", 0, 0), ("pass", 1, 0),
    ("hop2", 5, 0), ("loads",), ("hidden",), ("pass", 2, 0), ("hop2", 3, 0), ("hop2", 1, 0),
    ("hop1", 1, 1), ("square", 4, 0), ("gather", 4), ("fwd", 0, 0), ("hop2", 0, 0), ("fwd", 1, 0),
    ("square", 5, 0), ("hop1", 2, 1), ("gather", 5), ("fwd", 2, 0), ("fwd", 0, 1), ("pass", 1, 1),
    ("core", 4, 0), ("pass", 0, 0), ("square", 3, 0), ("hop1", 1, 2), ("sum1", 1, 1),
    ("gather", 3), ("sum1", 0, 1), ("pass", 2, 1), ("fwd", 2, 1), ("sum1", 1, 0), ("fwd", 3, 0),
    ("hop2", 2, 0), ("hop1", 2, 2), ("sum1", 1, 3), ("pass", 4, 0), ("fwd", 4, 0), ("core", 5, 0),
    ("sum1", 2, 2), ("core", 4, 1), ("sum1", 0, 3), ("sum1", 0, 2), ("sumz", 4, 3),
    ("pass", 5, 0), ("hop2", 1, 1), ("hop2", 2, 1), ("fwd", 5, 0), ("sumz", 5, 3), ("pass", 3, 0),
    ("hop2", 1, 2), ("sum1", 2, 3), ("sum1", 1, 2), ("sumz", 3, 3), ("pass", 2, 2),
    ("hop1", 2, 3), ("core", 3, 0), ("square", 1, 2), ("pass", 0, 1), ("sum2", 0, 2),
    ("square", 0, 0), ("pass", 1, 2), ("sumz", 4, 2), ("square", 1, 1), ("pass", 3, 1),
    ("hop1", 1, 3), ("hop2", 2, 2), ("hop2", 2, 3), ("pass", 5, 1), ("square", 2, 0),
    ("sum2", 1, 1), ("sumz", 5, 2), ("sum2", 2, 2), ("hop2", 1, 3), ("pass", 4, 1),
    ("core", 4, 2), ("square", 2, 1), ("core", 5, 2), ("hcore",), ("core", 1, 1), ("hop1", 0, 1),
    ("square", 1, 0), ("core", 3, 1), ("sum2", 0, 3), ("sum2", 1, 3), ("sum2", 1, 2),
    ("sum1", 2, 1), ("square", 2, 2), ("core", 5, 1), ("hop1", 0, 2), ("sum2", 0, 1),
    ("sum2", 1, 0), ("sum2", 2, 3), ("sumz", 3, 2), ("square", 2, 3), ("total", 0, 2),
    ("hg", 2, 0), ("total", 1, 1), ("core", 1, 2), ("hg", 2, 1), ("core", 2, 2), ("core", 2, 1),
    ("square", 1, 3), ("hg", 1, 0), ("total", 2, 2), ("sumz", 4, 1), ("core", 2, 0),
    ("sum1", 2, 0), ("core", 2, 3), ("hop2", 0, 1), ("core", 1, 0), ("pass", 3, 2), ("hg", 3, 0),
    ("core", 1, 3), ("core", 3, 3), ("core", 0, 0), ("total", 0, 3), ("core", 3, 2), ("hg", 1, 1),
    ("total", 1, 2), ("total", 1, 3), ("pass", 0, 2), ("sumz", 5, 1), ("hop1", 0, 3),
    ("hg", 3, 1), ("wg", 2, 0), ("sum2", 2, 1), ("pass", 5, 2), ("sumz", 3, 1), ("hop2", 0, 2),
    ("wg", 3, 0), ("hg", 5, 0), ("sum1", 0, 0), ("total", 2, 3), ("hg", 5, 1), ("pass", 4, 2),
    ("square", 0, 1), ("sumz", 1, 3), ("core", 4, 3), ("line", 3), ("total", 0, 1),
    ("hop2", 0, 3), ("line", 5), ("line", 4), ("sum1", 5, 0), ("sumz", 0, 3), ("sum1", 3, 0),
    ("core", 5, 3), ("sum1", 4, 0), ("wg", 4, 0), ("sum2", 2, 0), ("core", 0, 1), ("total", 2, 1),
    ("sumz", 2, 3), ("wg", 5, 0), ("sumz", 1, 2), ("hg", 4, 0), ("sum2", 0, 0), ("square", 0, 2),
    ("core", 0, 2), ("sumz", 1, 1), ("hg", 4, 1), ("sumz", 0, 2), ("sum2", 5, 0),
    ("square", 0, 3), ("core", 0, 3), ("wg", 1, 0), ("sum2", 4, 0), ("sum2", 3, 0),
    ("sumz", 2, 2), ("sumz", 0, 1), ("wg", 0, 0), ("sumz", 2, 1), ("hg", 0, 0), ("endx", 5),
    ("hg", 0, 1), ("endz", 1), ("endx", 3), ("endx", 4), ("endz", 0), ("endz", 2),
)


def remote(src, dst, send, recv, device):
    return pltpu.make_async_remote_copy(
        src_ref=src,
        dst_ref=dst,
        send_sem=send,
        recv_sem=recv,
        device_id=device,
        device_id_type=pl.DeviceIdType.MESH,
    )


def chunk_columns(width):
    unit = width // 8
    at, spans = 0, []
    for _, units in CHUNKS:
        spans.append((at, units * unit))
        at += units * unit
    return spans


def f32(value):
    return value.astype(jnp.float32)


def fused_kernel(
    scale,
    gate_hbm, up_hbm, weight_hbm, mask_ref, grad_hbm,
    final, gate_grad, up_grad, weight_grad,
    gate, up, weight, cot, hidden, hidden_t, partial, acc,
    in_sem, weight_sem, hidden_send, hidden_recv,
    *scratch,
):
    d = lax.axis_index("dp")
    t = lax.axis_index("tensor")
    x = t % 2
    y = (t // 2) % 2
    z = t // 4
    ff, width = weight.shape
    tokens = gate.shape[0]
    bf16 = jnp.bfloat16
    spans = chunk_columns(width)

    mid = ((z + 1) // 2) % 2
    end = 1 - mid
    is_mid = mid == 1
    inner = mid * (3 - z) + end * (1 + z // 3)
    outer = mid * (z - 1) * 3
    far = end * (3 - z) + mid * (2 - z) * 3
    blocks = (z, inner, end * (3 - inner) + mid * outer, far)

    def along(level):
        return {"tensor": level * 4 + y * 2 + x}

    x_peer = {"tensor": z * 4 + y * 2 + (1 - x)}
    y_peer = {"tensor": z * 4 + (1 - y) * 2 + x}
    core_peer = {"dp": 1 - d}
    inner_peer, outer_peer = along(inner), along(outer)

    loads = [
        pltpu.make_async_copy(gate_hbm, gate, in_sem.at[0]),
        pltpu.make_async_copy(up_hbm, up, in_sem.at[1]),
        pltpu.make_async_copy(grad_hbm, cot.at[d, z, y, x], in_sem.at[2]),
    ]
    weight_loads = {}
    for c, (at, size) in enumerate(spans):
        cols = pl.ds(at, size)
        weight_loads[c] = pltpu.make_async_copy(
            weight_hbm.at[:, cols], weight.at[:, cols], weight_sem.at[c]
        )
    for copy in loads:
        copy.start()
    for c in FORWARD:
        weight_loads[c].start()

    barrier = pltpu.get_barrier_semaphore()
    for peer in (x_peer, y_peer, core_peer, inner_peer):
        pl.semaphore_signal(barrier, inc=1, device_id=peer, device_id_type=pl.DeviceIdType.MESH)

    @pl.when(is_mid)
    def _():
        pl.semaphore_signal(
            barrier, inc=1, device_id=outer_peer, device_id_type=pl.DeviceIdType.MESH
        )

    pl.semaphore_wait(barrier, 4 + mid)

    hidden_core = remote(
        hidden_t.at[d], hidden_t.at[d], hidden_send.at[0], hidden_recv.at[0], core_peer
    )
    sent = []
    sent_mid = []

    def go(copy):
        copy.start()
        sent.append(copy)
        return copy

    class Chunk:
        pass

    def both_halves(chunk):
        return ((0, x_peer, y_peer, chunk.halves[0]), (1, y_peer, x_peer, chunk.halves[1]))

    chunks = []
    for c, (kind, _) in enumerate(CHUNKS):
        chunk = Chunk()
        at, size = spans[c]
        chunk.kind, chunk.at, chunk.size = kind, at, size
        chunk.cols = pl.ds(at, size)
        chunk.halves = (pl.ds(at, size // 2), pl.ds(at + size // 2, size // 2))
        chunk.first, chunk.second, chunk.along, chunk.send, chunk.recv = scratch[
            CHUNK_SCRATCH * c : CHUNK_SCRATCH * (c + 1)
        ]
        chunk.hop1, chunk.hop2, chunk.core, chunk.sum1, chunk.sum2 = {}, {}, {}, {}, {}
        chunks.append(chunk)


    def piece(chunk, b):
        if chunk.kind == "z":
            return cot.at[d, b, y, x, :, chunk.cols]
        return cot.at[d, b, :, :, :, chunk.cols]

    def gather_z(chunk):
        own = piece(chunk, z)
        src = grad_hbm.at[:, chunk.cols] if chunk.kind == "z" else own
        go(remote(src, own, chunk.send.at[36], chunk.recv.at[36 + end], inner_peer))

        @pl.when(is_mid)
        def _():
            remote(src, own, chunk.send.at[37], chunk.recv.at[36], outer_peer).start()

        sent_mid.append(remote(src, own, chunk.send.at[37], chunk.recv.at[36], outer_peer))

    def pass_z(chunk, s):
        block = piece(chunk, blocks[s + 1])
        remote(block, block, chunk.send.at[36], chunk.recv.at[36 + s], inner_peer).wait_recv()
        to, slot = ((outer_peer, 1), (inner_peer, 2), (outer_peer, 2))[s]
        copy = remote(block, block, chunk.send.at[38 + s], chunk.recv.at[36 + slot], to)

        @pl.when(is_mid)
        def _():
            copy.start()

        sent_mid.append(copy)

    def hop1(chunk, k):
        for h, near, _, half in both_halves(chunk):
            dst = cot.at[d, blocks[k], y, x, :, half]
            src = grad_hbm.at[:, half] if k == 0 else dst
            n = 2 * k + h
            chunk.hop1[k, h] = go(remote(src, dst, chunk.send.at[n], chunk.recv.at[n], near))

    def hop2(chunk, k):
        for h in range(2):
            chunk.hop1[k, h].wait_recv()
        for h, _, other, half in both_halves(chunk):
            ref = (cot.at[d, blocks[k], y, :, :, half], cot.at[d, blocks[k], :, x, :, half])[h]
            n = 8 + 2 * k + h
            chunk.hop2[k, h] = go(remote(ref, ref, chunk.send.at[n], chunk.recv.at[n], other))

    def square(chunk, k):
        for h in range(2):
            chunk.hop2[k, h].wait_recv()

    def to_core(chunk, k):
        size = chunk.size // 2
        cols = pl.ds(pl.multiple_of(chunk.at + (1 - d) * size, 256), size)
        ref = cot.at[d, blocks[k], :, :, :, cols]
        chunk.core[k] = go(
            remote(ref, ref, chunk.send.at[16 + k], chunk.recv.at[16 + k], core_peer)
        )

    def sum1(chunk, k):
        for h, near, _, half in both_halves(chunk):
            src = (
                partial.at[blocks[k], :, 1 - x, :, half],
                partial.at[blocks[k], 1 - y, :, :, half],
            )[h]
            n = 20 + 2 * k + h
            chunk.sum1[k, h] = go(
                remote(src, chunk.first.at[h, k], chunk.send.at[n], chunk.recv.at[n], near)
            )

    def sum2(chunk, k):
        for h, _, other, half in both_halves(chunk):
            chunk.sum1[k, h].wait_recv()
            row, column, there = ((1 - y, x, 1 - y), (y, 1 - x, 1 - x))[h]
            total = f32(partial[blocks[k], row, column, :, half]) + f32(chunk.first[h, k, there])
            partial[blocks[k], row, column, :, half] = total.astype(bf16)
            n = 28 + 2 * k + h
            chunk.sum2[k, h] = go(
                remote(
                    partial.at[blocks[k], row, column, :, half], chunk.second.at[h, k],
                    chunk.send.at[n], chunk.recv.at[n], other,
                )
            )

    def own_total(chunk, k, h):
        mine = f32(partial[blocks[k], y, x, :, chunk.halves[h]])
        return mine + f32(chunk.first[h, k, (y, x)[h]]) + f32(chunk.second[h, k])

    def square_total(chunk, k):
        for h in range(2):
            chunk.sum2[k, h].wait_recv()
            partial[blocks[k], y, x, :, chunk.halves[h]] = own_total(chunk, k, h).astype(bf16)

    def term(chunk, k):
        if chunk.kind == "z":
            return partial.at[blocks[k], y, x, :, chunk.cols]
        return partial.at[blocks[k], :, :, :, chunk.cols]

    def arrived(chunk, slot):
        ref = chunk.along.at[slot]
        remote(ref, ref, chunk.send.at[41], chunk.recv.at[41 + slot], inner_peer).wait_recv()

    def add_term(chunk, k, slots):
        if chunk.kind == "z":
            total = f32(partial[blocks[k], y, x, :, chunk.cols])
            for slot in slots:
                total = total + f32(chunk.along[slot])
            partial[blocks[k], y, x, :, chunk.cols] = total.astype(bf16)
            return

        wide = 256

        def step(i, _):
            here = pl.ds(pl.multiple_of(i * wide, wide), wide)
            cols = pl.ds(pl.multiple_of(chunk.at + i * wide, wide), wide)
            total = f32(partial[blocks[k], :, :, :, cols])
            for slot in slots:
                total = total + f32(chunk.along[slot, :, :, :, here])
            partial[blocks[k], :, :, :, cols] = total.astype(bf16)
            return 0

        lax.fori_loop(0, chunk.size // wide, step, 0)

    def sum_z(chunk, k):
        @pl.when(is_mid)
        def _():
            arrived(chunk, k)
            add_term(chunk, k, (k,))

        slot = (None, 4 * mid, end, 2 + end)[k]
        to = along(end * inner + mid * outer) if k == 2 else inner_peer
        ref = term(chunk, k)
        go(remote(ref, chunk.along.at[slot], chunk.send.at[41 + k], chunk.recv.at[41 + slot], to))

    def line_total(chunk):
        arrived(chunk, 0)

        @pl.when(is_mid)
        def _():
            arrived(chunk, 4)
            add_term(chunk, 0, (0, 4))

        @pl.when(end == 1)
        def _():
            add_term(chunk, 0, (0,))

    def finish_z(chunk):
        arrived(chunk, 0)
        size = chunk.size // 2

        @pl.when(is_mid)
        def _():
            arrived(chunk, 4)

        for h in range(2):
            chunk.sum2[0, h].wait_recv()
            here = pl.ds(h * size, size)
            total = own_total(chunk, 0, h) + f32(chunk.along[0, :, here])

            @pl.when(is_mid)
            def _():
                final[:, chunk.halves[h]] = (total + f32(chunk.along[4, :, here])).astype(bf16)

            @pl.when(end == 1)
            def _():
                final[:, chunk.halves[h]] = total.astype(bf16)

    def finish_x(chunk):
        for h in range(2):
            chunk.sum2[0, h].wait_recv()
            final[:, chunk.halves[h]] = own_total(chunk, 0, h).astype(bf16)

    graded = [0, 0]

    def hidden_step(step, _):
        cols = pl.ds(pl.multiple_of(step * 128, 128), 128)
        g = f32(gate[:, cols])
        u = f32(up[:, cols])
        value = g * jax.nn.sigmoid(g) * u
        hidden[:, cols] = value.astype(bf16)
        hidden_t[d, cols, :] = value.T.astype(bf16)
        return 0

    def forward(chunk, i):
        base = chunk.at + i * STEP
        cols = pl.ds(base, STEP)
        for b in range(ff // BLOCK):
            keep = jnp.concatenate(
                [
                    jnp.full((16, BLOCK), f32(mask_ref[b, base // BLOCK + c])).astype(bf16)
                    for c in range(STEP // BLOCK)
                ],
                axis=1,
            )
            for r in range(BLOCK // 16):
                rows = pl.ds(b * BLOCK + r * 16, 16)
                weight[rows, cols] = weight[rows, cols] * keep
        part = jnp.dot(hidden[...], weight[:, cols], preferred_element_type=jnp.float32)
        partial[:, :, :, :, cols] = part.astype(bf16).reshape(partial.shape[:4] + (STEP,))

    def hidden_grad(chunk, part):
        begin, close = graded[part] == 0, graded[part] == len(CHUNKS) - 1
        graded[part] += 1
        wide = 512

        def step(i, _):
            rows = pl.ds(pl.multiple_of(i * wide, wide), wide)
            back = lax.dot_general(
                cot[d, :, :, :, :, chunk.cols].reshape(tokens, chunk.size),
                weight[rows, chunk.cols],
                (((1,), (1,)), ((), ())),
                preferred_element_type=jnp.float32,
            )
            if not begin:
                back = back + acc[:, rows]
            if not close:
                acc[:, rows] = back
                return 0
            g = f32(gate[:, rows])
            u = f32(up[:, rows])
            s = jax.nn.sigmoid(g)
            gate_grad[:, rows] = (back * u * s * (1.0 + g * (1.0 - s))).astype(bf16)
            up_grad[:, rows] = (back * (g * s)).astype(bf16)
            return 0

        count = ff // wide // 2
        lax.fori_loop(part * count, (part + 1) * count, step, 0)

    def weight_half(chunk):
        size = chunk.size // 2
        base = pl.multiple_of(chunk.at + d * size, 256)
        cols = pl.ds(base, size)
        total = jnp.zeros((ff, size), jnp.float32)
        for core in range(2):
            total = total + jnp.dot(
                hidden_t[core],
                cot[core, :, :, :, :, cols].reshape(tokens, size),
                preferred_element_type=jnp.float32,
            )
        for b in range(ff // BLOCK):
            for c in range(size // BLOCK):
                keep = f32(mask_ref[b, chunk.at // BLOCK + d * (size // BLOCK) + c]) * scale
                block = total[b * BLOCK : (b + 1) * BLOCK, c * BLOCK : (c + 1) * BLOCK]
                at = pl.ds(pl.multiple_of(base + c * BLOCK, BLOCK), BLOCK)
                weight_grad[pl.ds(b * BLOCK, BLOCK), at] = (block * keep).astype(bf16)
        chunk.half = go(
            remote(
                weight_grad.at[:, cols], weight_grad.at[:, cols], chunk.send.at[46],
                chunk.recv.at[46], core_peer,
            )
        )

    def do_loads():
        loads[0].wait()
        loads[1].wait()

    def do_hidden():
        lax.fori_loop(0, ff // 128, hidden_step, 0)
        hidden_core.start()

    def do_forward(c, i):
        if i == 0:
            weight_loads[c].wait()
        forward(chunks[c], i)

    def do_weight(c, _):
        for k in range(4):
            chunks[c].core[k].wait_recv()
        weight_half(chunks[c])

    actions = {
        "loads": do_loads,
        "hidden": do_hidden,
        "own": lambda: loads[2].wait(),
        "hcore": lambda: hidden_core.wait_recv(),
        "fwd": do_forward,
        "wg": do_weight,
        "hg": lambda c, part: hidden_grad(chunks[c], part),
        "gather": lambda c: gather_z(chunks[c]),
        "pass": lambda c, k: pass_z(chunks[c], k),
        "hop1": lambda c, k: hop1(chunks[c], k),
        "hop2": lambda c, k: hop2(chunks[c], k),
        "square": lambda c, k: square(chunks[c], k),
        "core": lambda c, k: to_core(chunks[c], k),
        "sum1": lambda c, k: sum1(chunks[c], k),
        "sum2": lambda c, k: sum2(chunks[c], k),
        "total": lambda c, k: square_total(chunks[c], k),
        "sumz": lambda c, k: sum_z(chunks[c], k),
        "line": lambda c: line_total(chunks[c]),
        "endz": lambda c: finish_z(chunks[c]),
        "endx": lambda c: finish_x(chunks[c]),
    }
    for name, *args in PLAN:
        actions[name](*args)

    for chunk in chunks:
        chunk.half.wait_recv()
    for copy in sent:
        copy.wait_send()

    @pl.when(is_mid)
    def _():
        for copy in sent_mid:
            copy.wait_send()

    hidden_core.wait_send()


def keep_in_hbm(array):
    return pltpu.with_memory_space_constraint(array, pltpu.HBM)


def chunk_scratch(rows, width):
    dma = pltpu.SemaphoreType.DMA
    bf16 = jnp.bfloat16
    scratch = []
    for (kind, _), (_, size) in zip(CHUNKS, chunk_columns(width)):
        levels = 4 if kind == "z" else 1
        held = (rows,) if kind == "z" else (2, 2, rows)
        scratch += [
            pltpu.VMEM((2, levels, 2, rows, size // 2), bf16),
            pltpu.VMEM((2, levels, rows, size // 2), bf16),
            pltpu.VMEM((5,) + held + (size,), bf16),
            dma((47,)),
            dma((47,)),
        ]
    return scratch


def fused(gate_pre, up_pre, down_weight, block_mask, out_grad):
    tokens, ff = gate_pre.shape
    rows, width = out_grad.shape
    scale = 1.0 / math.sqrt(tokens * 2)
    hbm = pl.BlockSpec(memory_space=pl.ANY)
    bf16 = jnp.bfloat16
    dma = pltpu.SemaphoreType.DMA
    results = pl.pallas_call(
        functools.partial(fused_kernel, scale),
        out_shape=(
            pltpu.VMEM((rows, width), bf16),
            pltpu.VMEM((tokens, ff), bf16),
            pltpu.VMEM((tokens, ff), bf16),
            pltpu.VMEM((ff, width), bf16),
        ),
        in_specs=[hbm, hbm, hbm, pl.BlockSpec(memory_space=pltpu.SMEM), hbm],
        out_specs=(pl.BlockSpec(memory_space=pltpu.VMEM),) * 4,
        scratch_shapes=[
            pltpu.VMEM((tokens, ff), bf16),
            pltpu.VMEM((tokens, ff), bf16),
            pltpu.VMEM((ff, width), bf16),
            pltpu.VMEM((2, 4, 2, 2, rows, width), bf16),
            pltpu.VMEM((tokens, ff), bf16),
            pltpu.VMEM((2, ff, tokens), bf16),
            pltpu.VMEM((4, 2, 2, rows, width), bf16),
            pltpu.VMEM((tokens, ff), jnp.float32),
            dma((3,)),
            dma((len(CHUNKS),)),
            dma((1,)),
            dma((1,)),
        ]
        + chunk_scratch(rows, width),
        compiler_params=pltpu.CompilerParams(
            collective_id=0, has_side_effects=True, vmem_limit_bytes=50 * 2**20
        ),
        cost_estimate=pl.CostEstimate(
            flops=8 * tokens * ff * width, bytes_accessed=40 * 2**20, transcendentals=2 * tokens * ff
        ),
    )(*(keep_in_hbm(a) for a in (gate_pre, up_pre, down_weight)), block_mask, keep_in_hbm(out_grad))
    return hand_on(results)


def hand_on_kernel(arrays, *refs):
    srcs, dsts, store_sem = refs[:arrays], refs[arrays : 2 * arrays], refs[2 * arrays]
    stores = [
        pltpu.make_async_copy(src, dst, store_sem.at[n])
        for n, (src, dst) in enumerate(zip(srcs, dsts))
    ]
    for store in stores:
        store.start()
    for store in stores:
        store.wait()


def hand_on(arrays):
    return pl.pallas_call(
        functools.partial(hand_on_kernel, len(arrays)),
        out_shape=tuple(jax.ShapeDtypeStruct(a.shape, a.dtype) for a in arrays),
        in_specs=[pl.BlockSpec(memory_space=pltpu.VMEM)] * len(arrays),
        out_specs=(pl.BlockSpec(memory_space=pl.ANY),) * len(arrays),
        scratch_shapes=[pltpu.SemaphoreType.DMA((len(arrays),))],
        compiler_params=pltpu.CompilerParams(vmem_limit_bytes=2 * 2**20),
    )(*(pltpu.with_memory_space_constraint(a, pltpu.VMEM) for a in arrays))


def local(gate_pre, up_pre, down_weight, block_mask, out_grad):
    blk_rows, blk_cols = block_mask.shape
    ff_local, width = down_weight.shape
    masked = (
        down_weight.reshape(blk_rows, 128, blk_cols, 128)
        * block_mask.astype(jnp.bfloat16)[:, None, :, None]
    ).reshape(ff_local, width)
    gate_val = gate_pre.astype(jnp.float32)
    up_val = up_pre.astype(jnp.float32)
    sigmoid_gate = jax.nn.sigmoid(gate_val)
    silu_gate = gate_val * sigmoid_gate
    hidden = (silu_gate * up_val).astype(jnp.bfloat16)
    layer_out = lax.psum_scatter(
        jnp.dot(hidden, masked, preferred_element_type=jnp.float32),
        "tensor",
        scatter_dimension=0,
        tiled=True,
    ).astype(jnp.bfloat16)
    cot_rows = lax.all_gather(out_grad, "tensor", axis=0, tiled=True)
    hidden_grad = lax.dot_general(
        cot_rows, masked, (((1,), (1,)), ((), ())), preferred_element_type=jnp.float32
    )
    gate_grad = (
        hidden_grad * up_val * sigmoid_gate * (1.0 + gate_val * (1.0 - sigmoid_gate))
    ).astype(jnp.bfloat16)
    up_grad = (hidden_grad * silu_gate).astype(jnp.bfloat16)
    tokens_all = out_grad.shape[0] * lax.axis_size("tensor") * lax.axis_size("dp")
    grad_scale = 1.0 / math.sqrt(tokens_all)
    partial_grad = (
        lax.dot_general(
            hidden, cot_rows, (((0,), (0,)), ((), ())), preferred_element_type=jnp.float32
        )
        * grad_scale
    )
    blocked = (
        partial_grad.reshape(blk_rows, 128, blk_cols, 128)
        * block_mask.astype(jnp.float32)[:, None, :, None]
    )
    summed = lax.psum(blocked.reshape(ff_local, width), "dp")
    weight_grad = summed.astype(jnp.bfloat16)
    return (layer_out, gate_grad, up_grad, weight_grad)


def solution(mesh):
    grouped = mesh.shape["dp"] == 2 and mesh.shape["tensor"] == 16
    return jax.shard_map(
        fused if grouped else local,
        mesh=mesh,
        in_specs=(
            P("dp", "tensor"),
            P("dp", "tensor"),
            P("tensor", None),
            P("tensor", None),
            P(("dp", "tensor"), None),
        ),
        out_specs=(
            P(("dp", "tensor"), None),
            P("dp", "tensor"),
            P("dp", "tensor"),
            P("tensor", None),
        ),
        check_vma=False,
    )
```

```python
import functools
import math

import jax
import jax.numpy as jnp
from jax import lax
from jax.experimental import pallas as pl
from jax.experimental.pallas import tpu as pltpu
from jax.sharding import PartitionSpec as P

BLOCK = 128
STEP = 512
CHUNKS = (("z", 1), ("z", 2), ("z", 2), ("x", 1), ("x", 1), ("x", 1))
CHUNK_SCRATCH = 5


FORWARD = (1, 4, 0, 5, 2, 3)
MID_PLAN = (
    ("hop1", 3, 0), ("hop1", 4, 0), ("gather", 0), ("gather", 2), ("hop1", 5, 0), ("hop1", 1, 0),
    ("gather", 1), ("hop1", 0, 0), ("hop1", 2, 0), ("own",), ("hop2", 3, 0), ("pass", 0, 0),
    ("pass", 0, 1), ("hop1", 0, 1), ("hop2", 5, 0), ("hop2", 1, 0), ("pass", 2, 0),
    ("pass", 1, 1), ("hop1", 0, 2), ("pass", 1, 0), ("hop1", 1, 1), ("hop2", 4, 0),
    ("square", 3, 0), ("hop1", 2, 1), ("pass", 0, 2), ("pass", 2, 1), ("hop1", 2, 2), ("loads",),
    ("gather", 3), ("hidden",), ("square", 5, 0), ("pass", 1, 2), ("square", 1, 0),
    ("hop2", 0, 1), ("hop2", 2, 0), ("fwd", 1, 0), ("gather", 5), ("hop1", 0, 3), ("hop2", 0, 0),
    ("pass", 2, 2), ("core", 5, 0), ("fwd", 4, 0), ("fwd", 0, 0), ("hop1", 1, 2), ("fwd", 5, 0),
    ("square", 4, 0), ("pass", 3, 1), ("hop2", 2, 2), ("hcore",), ("hop1", 2, 3), ("core", 4, 0),
    ("pass", 3, 0), ("fwd", 2, 0), ("fwd", 2, 1), ("hop2", 1, 1), ("hop1", 1, 3),
    ("square", 0, 0), ("pass", 5, 0), ("pass", 5, 1), ("fwd", 1, 1), ("hop2", 2, 1),
    ("pass", 4, 1), ("hop2", 0, 3), ("pass", 3, 2), ("sumz", 4, 3), ("hop2", 2, 3), ("gather", 4),
    ("square", 1, 1), ("core", 3, 3), ("hop2", 1, 3), ("sum1", 0, 3), ("sum1", 2, 1),
    ("pass", 5, 2), ("square", 2, 0), ("hop2", 1, 2), ("square", 2, 3), ("hg", 5, 0),
    ("sum1", 2, 3), ("sum2", 0, 3), ("hop2", 0, 2), ("fwd", 3, 0), ("sum1", 0, 2), ("sum1", 1, 1),
    ("sumz", 3, 3), ("square", 2, 2), ("sum1", 1, 2), ("hg", 5, 1), ("sum2", 2, 1),
    ("sumz", 5, 3), ("square", 1, 3), ("core", 0, 0), ("core", 1, 0), ("square", 2, 1),
    ("square", 0, 3), ("square", 0, 1), ("hg", 2, 0), ("pass", 4, 0), ("core", 1, 3),
    ("square", 1, 2), ("sum1", 0, 1), ("total", 0, 3), ("sum1", 1, 3), ("sum1", 2, 0),
    ("core", 5, 1), ("sumz", 4, 1), ("core", 5, 3), ("hg", 1, 0), ("core", 2, 3), ("hg", 3, 0),
    ("sumz", 4, 2), ("core", 4, 1), ("sumz", 3, 1), ("square", 0, 2), ("sumz", 3, 2),
    ("hg", 2, 1), ("core", 2, 0), ("core", 2, 2), ("hg", 3, 1), ("hg", 0, 0), ("core", 2, 1),
    ("core", 0, 2), ("core", 1, 1), ("core", 1, 2), ("core", 3, 1), ("sum2", 0, 2),
    ("sumz", 5, 2), ("sum2", 2, 3), ("pass", 4, 2), ("core", 3, 0), ("hg", 4, 0), ("core", 3, 2),
    ("sumz", 5, 1), ("sum2", 1, 2), ("sum2", 1, 3), ("core", 4, 3), ("core", 4, 2),
    ("core", 0, 3), ("sum2", 0, 1), ("sumz", 0, 3), ("sum1", 2, 2), ("total", 2, 1), ("line", 4),
    ("sum1", 4, 0), ("sum1", 1, 0), ("hg", 0, 1), ("hg", 1, 1), ("sum2", 1, 1), ("wg", 2, 0),
    ("total", 1, 3), ("sumz", 1, 3), ("wg", 4, 0), ("total", 1, 2), ("total", 0, 2), ("line", 3),
    ("total", 2, 3), ("sum1", 3, 0), ("total", 0, 1), ("sum2", 2, 2), ("core", 0, 1),
    ("sumz", 2, 3), ("core", 5, 2), ("wg", 1, 0), ("sum1", 0, 0), ("line", 5), ("sum1", 5, 0),
    ("sum2", 2, 0), ("sum2", 1, 0), ("sumz", 0, 1), ("sumz", 2, 1), ("sumz", 0, 2),
    ("sum2", 4, 0), ("sumz", 1, 2), ("sum2", 3, 0), ("total", 1, 1), ("wg", 0, 0),
    ("total", 2, 2), ("sumz", 2, 2), ("sumz", 1, 1), ("wg", 3, 0), ("sum2", 0, 0), ("sum2", 5, 0),
    ("wg", 5, 0), ("hg", 4, 1), ("endz", 0), ("endz", 1), ("endz", 2), ("endx", 4), ("endx", 3),
    ("endx", 5),
)
END_PLAN = (
    ("hop1", 3, 0), ("gather", 0), ("hop1", 5, 0), ("hop1", 1, 0), ("own",), ("hop1", 0, 0),
    ("gather", 1), ("hop1", 4, 0), ("gather", 2), ("hop1", 2, 0), ("loads",), ("hidden",),
    ("hop2", 5, 0), ("hop2", 3, 0), ("fwd", 4, 0), ("hop2", 1, 0), ("sumz", 4, 3), ("hop2", 4, 0),
    ("pass", 0, 0), ("fwd", 2, 0), ("fwd", 2, 1), ("pass", 2, 0), ("sum1", 2, 3), ("fwd", 0, 0),
    ("square", 5, 0), ("pass", 1, 0), ("sum1", 0, 2), ("square", 3, 0), ("hop1", 1, 1),
    ("pass", 0, 1), ("gather", 3), ("gather", 5), ("hop1", 0, 1), ("pass", 2, 1), ("fwd", 3, 0),
    ("core", 3, 0), ("hop1", 0, 2), ("hcore",), ("square", 4, 0), ("hop2", 2, 0), ("fwd", 5, 0),
    ("hop1", 2, 2), ("gather", 4), ("pass", 1, 1), ("sum2", 0, 2), ("hop2", 1, 1), ("hop1", 1, 2),
    ("pass", 3, 0), ("pass", 0, 2), ("hop2", 0, 0), ("hop2", 0, 1), ("sum1", 0, 3),
    ("pass", 1, 2), ("hop1", 1, 3), ("sumz", 5, 3), ("sumz", 4, 2), ("sum1", 2, 2),
    ("square", 0, 1), ("hop2", 1, 2), ("sum2", 2, 3), ("square", 1, 0), ("hop2", 1, 3),
    ("sumz", 3, 3), ("square", 2, 0), ("sumz", 3, 2), ("pass", 2, 2), ("fwd", 1, 0),
    ("pass", 3, 1), ("core", 1, 0), ("hop1", 0, 3), ("sumz", 4, 1), ("fwd", 1, 1), ("pass", 5, 0),
    ("sum1", 1, 3), ("sum1", 0, 1), ("square", 1, 1), ("hop1", 2, 1), ("square", 1, 2),
    ("pass", 5, 1), ("sumz", 5, 2), ("total", 0, 2), ("core", 3, 2), ("hop2", 0, 3),
    ("hop2", 0, 2), ("sum2", 1, 3), ("square", 1, 3), ("core", 1, 2), ("sum1", 1, 2),
    ("sumz", 3, 1), ("sum2", 0, 3), ("hg", 1, 0), ("core", 5, 1), ("core", 1, 1), ("hop1", 2, 3),
    ("total", 2, 3), ("hop2", 2, 1), ("square", 0, 2), ("sum2", 2, 2), ("pass", 3, 2),
    ("core", 5, 2), ("total", 1, 3), ("hg", 3, 0), ("hg", 3, 1), ("core", 1, 3), ("sum2", 1, 2),
    ("pass", 5, 2), ("pass", 4, 0), ("hop2", 2, 2), ("hg", 5, 0), ("core", 5, 0), ("hg", 5, 1),
    ("square", 0, 0), ("sum1", 1, 1), ("sum2", 0, 1), ("total", 0, 3), ("hop2", 2, 3),
    ("core", 3, 1), ("core", 2, 0), ("sumz", 0, 3), ("square", 0, 3), ("core", 0, 3),
    ("core", 5, 3), ("core", 0, 1), ("sumz", 1, 3), ("sumz", 2, 3), ("core", 0, 2),
    ("core", 3, 3), ("sumz", 5, 1), ("wg", 1, 0), ("sum1", 2, 1), ("total", 2, 2), ("sumz", 2, 2),
    ("hg", 0, 0), ("core", 4, 1), ("sum1", 2, 0), ("square", 2, 1), ("hg", 0, 1), ("core", 0, 0),
    ("wg", 3, 0), ("wg", 5, 0), ("wg", 0, 0), ("core", 2, 1), ("sum1", 1, 0), ("square", 2, 2),
    ("total", 1, 2), ("total", 0, 1), ("sumz", 0, 2), ("line", 3), ("sum2", 1, 1), ("sum1", 0, 0),
    ("sum1", 3, 0), ("pass", 4, 1), ("square", 2, 3), ("core", 2, 2), ("core", 2, 3),
    ("sumz", 0, 1), ("line", 4), ("hg", 1, 1), ("sum2", 2, 1), ("sumz", 1, 2), ("line", 5),
    ("sum1", 5, 0), ("core", 4, 2), ("sum1", 4, 0), ("wg", 2, 0), ("hg", 2, 0), ("pass", 4, 2),
    ("sum2", 2, 0), ("core", 4, 0), ("total", 1, 1), ("sumz", 1, 1), ("core", 4, 3),
    ("sum2", 1, 0), ("hg", 4, 0), ("sum2", 3, 0), ("total", 2, 1), ("sum2", 0, 0), ("sumz", 2, 1),
    ("wg", 4, 0), ("sum2", 5, 0), ("sum2", 4, 0), ("hg", 4, 1), ("hg", 2, 1), ("endz", 1),
    ("endz", 2), ("endx", 3), ("endx", 5), ("endz", 0), ("endx", 4),
)


def remote(src, dst, send, recv, device):
    return pltpu.make_async_remote_copy(
        src_ref=src,
        dst_ref=dst,
        send_sem=send,
        recv_sem=recv,
        device_id=device,
        device_id_type=pl.DeviceIdType.MESH,
    )


def chunk_columns(width):
    unit = width // 8
    at, spans = 0, []
    for _, units in CHUNKS:
        spans.append((at, units * unit))
        at += units * unit
    return spans


def f32(value):
    return value.astype(jnp.float32)


def fused_kernel(
    scale,
    gate_hbm, up_hbm, weight_hbm, mask_ref, grad_hbm,
    final, gate_grad, up_grad, weight_grad,
    gate, up, weight, cot, hidden, hidden_t, partial, acc,
    in_sem, weight_sem, hidden_send, hidden_recv,
    *scratch,
):
    d = lax.axis_index("dp")
    t = lax.axis_index("tensor")
    x = t % 2
    y = (t // 2) % 2
    z = t // 4
    ff, width = weight.shape
    tokens = gate.shape[0]
    bf16 = jnp.bfloat16
    spans = chunk_columns(width)

    mid = ((z + 1) // 2) % 2
    end = 1 - mid
    is_mid = mid == 1
    inner = mid * (3 - z) + end * (1 + z // 3)
    outer = mid * (z - 1) * 3
    far = end * (3 - z) + mid * (2 - z) * 3
    blocks = (z, inner, end * (3 - inner) + mid * outer, far)

    def along(level):
        return {"tensor": level * 4 + y * 2 + x}

    x_peer = {"tensor": z * 4 + y * 2 + (1 - x)}
    y_peer = {"tensor": z * 4 + (1 - y) * 2 + x}
    core_peer = {"dp": 1 - d}
    inner_peer, outer_peer = along(inner), along(outer)

    loads = [
        pltpu.make_async_copy(gate_hbm, gate, in_sem.at[0]),
        pltpu.make_async_copy(up_hbm, up, in_sem.at[1]),
        pltpu.make_async_copy(grad_hbm, cot.at[d, z, y, x], in_sem.at[2]),
    ]
    weight_loads = {}
    for c, (at, size) in enumerate(spans):
        cols = pl.ds(at, size)
        weight_loads[c] = pltpu.make_async_copy(
            weight_hbm.at[:, cols], weight.at[:, cols], weight_sem.at[c]
        )
    for copy in loads:
        copy.start()
    for c in FORWARD:
        weight_loads[c].start()

    barrier = pltpu.get_barrier_semaphore()
    for peer in (x_peer, y_peer, core_peer, inner_peer):
        pl.semaphore_signal(barrier, inc=1, device_id=peer, device_id_type=pl.DeviceIdType.MESH)

    @pl.when(is_mid)
    def _():
        pl.semaphore_signal(
            barrier, inc=1, device_id=outer_peer, device_id_type=pl.DeviceIdType.MESH
        )

    pl.semaphore_wait(barrier, 4 + mid)

    def run(is_mid, plan):
        mid = int(is_mid)
        end = 1 - mid

        hidden_core = remote(
            hidden_t.at[d], hidden_t.at[d], hidden_send.at[0], hidden_recv.at[0], core_peer
        )
        sent = []

        def go(copy):
            copy.start()
            sent.append(copy)
            return copy

        class Chunk:
            pass

        def both_halves(chunk):
            return ((0, x_peer, y_peer, chunk.halves[0]), (1, y_peer, x_peer, chunk.halves[1]))

        chunks = []
        for c, (kind, _) in enumerate(CHUNKS):
            chunk = Chunk()
            at, size = spans[c]
            chunk.kind, chunk.at, chunk.size = kind, at, size
            chunk.cols = pl.ds(at, size)
            chunk.halves = (pl.ds(at, size // 2), pl.ds(at + size // 2, size // 2))
            chunk.first, chunk.second, chunk.along, chunk.send, chunk.recv = scratch[
                CHUNK_SCRATCH * c : CHUNK_SCRATCH * (c + 1)
            ]
            chunk.hop1, chunk.hop2, chunk.core, chunk.sum1, chunk.sum2 = {}, {}, {}, {}, {}
            chunks.append(chunk)


        def piece(chunk, b):
            if chunk.kind == "z":
                return cot.at[d, b, y, x, :, chunk.cols]
            return cot.at[d, b, :, :, :, chunk.cols]

        def gather_z(chunk):
            own = piece(chunk, z)
            src = grad_hbm.at[:, chunk.cols] if chunk.kind == "z" else own
            go(remote(src, own, chunk.send.at[36], chunk.recv.at[36 + end], inner_peer))

            if is_mid:
                go(remote(src, own, chunk.send.at[37], chunk.recv.at[36], outer_peer))

        def pass_z(chunk, s):
            block = piece(chunk, blocks[s + 1])
            remote(block, block, chunk.send.at[36], chunk.recv.at[36 + s], inner_peer).wait_recv()
            if not is_mid:
                return
            to, slot = ((outer_peer, 1), (inner_peer, 2), (outer_peer, 2))[s]
            copy = remote(block, block, chunk.send.at[38 + s], chunk.recv.at[36 + slot], to)

            go(copy)

        def hop1(chunk, k):
            for h, near, _, half in both_halves(chunk):
                dst = cot.at[d, blocks[k], y, x, :, half]
                src = grad_hbm.at[:, half] if k == 0 else dst
                n = 2 * k + h
                chunk.hop1[k, h] = go(remote(src, dst, chunk.send.at[n], chunk.recv.at[n], near))

        def hop2(chunk, k):
            for h in range(2):
                chunk.hop1[k, h].wait_recv()
            for h, _, other, half in both_halves(chunk):
                ref = (cot.at[d, blocks[k], y, :, :, half], cot.at[d, blocks[k], :, x, :, half])[h]
                n = 8 + 2 * k + h
                chunk.hop2[k, h] = go(remote(ref, ref, chunk.send.at[n], chunk.recv.at[n], other))

        def square(chunk, k):
            for h in range(2):
                chunk.hop2[k, h].wait_recv()

        def to_core(chunk, k):
            size = chunk.size // 2
            cols = pl.ds(pl.multiple_of(chunk.at + (1 - d) * size, 256), size)
            ref = cot.at[d, blocks[k], :, :, :, cols]
            chunk.core[k] = go(
                remote(ref, ref, chunk.send.at[16 + k], chunk.recv.at[16 + k], core_peer)
            )

        def sum1(chunk, k):
            for h, near, _, half in both_halves(chunk):
                src = (
                    partial.at[blocks[k], :, 1 - x, :, half],
                    partial.at[blocks[k], 1 - y, :, :, half],
                )[h]
                n = 20 + 2 * k + h
                chunk.sum1[k, h] = go(
                    remote(src, chunk.first.at[h, k], chunk.send.at[n], chunk.recv.at[n], near)
                )

        def sum2(chunk, k):
            for h, _, other, half in both_halves(chunk):
                chunk.sum1[k, h].wait_recv()
                row, column, there = ((1 - y, x, 1 - y), (y, 1 - x, 1 - x))[h]
                total = f32(partial[blocks[k], row, column, :, half]) + f32(chunk.first[h, k, there])
                partial[blocks[k], row, column, :, half] = total.astype(bf16)
                n = 28 + 2 * k + h
                chunk.sum2[k, h] = go(
                    remote(
                        partial.at[blocks[k], row, column, :, half], chunk.second.at[h, k],
                        chunk.send.at[n], chunk.recv.at[n], other,
                    )
                )

        def own_total(chunk, k, h):
            mine = f32(partial[blocks[k], y, x, :, chunk.halves[h]])
            return mine + f32(chunk.first[h, k, (y, x)[h]]) + f32(chunk.second[h, k])

        def square_total(chunk, k):
            for h in range(2):
                chunk.sum2[k, h].wait_recv()
                partial[blocks[k], y, x, :, chunk.halves[h]] = own_total(chunk, k, h).astype(bf16)

        def term(chunk, k):
            if chunk.kind == "z":
                return partial.at[blocks[k], y, x, :, chunk.cols]
            return partial.at[blocks[k], :, :, :, chunk.cols]

        def arrived(chunk, slot):
            ref = chunk.along.at[slot]
            remote(ref, ref, chunk.send.at[41], chunk.recv.at[41 + slot], inner_peer).wait_recv()

        def add_term(chunk, k, slots):
            if chunk.kind == "z":
                total = f32(partial[blocks[k], y, x, :, chunk.cols])
                for slot in slots:
                    total = total + f32(chunk.along[slot])
                partial[blocks[k], y, x, :, chunk.cols] = total.astype(bf16)
                return

            wide = 256

            def step(i, _):
                here = pl.ds(pl.multiple_of(i * wide, wide), wide)
                cols = pl.ds(pl.multiple_of(chunk.at + i * wide, wide), wide)
                total = f32(partial[blocks[k], :, :, :, cols])
                for slot in slots:
                    total = total + f32(chunk.along[slot, :, :, :, here])
                partial[blocks[k], :, :, :, cols] = total.astype(bf16)
                return 0

            lax.fori_loop(0, chunk.size // wide, step, 0)

        def sum_z(chunk, k):
            if is_mid:
                arrived(chunk, k)
                add_term(chunk, k, (k,))

            slot = (None, 4 * mid, end, 2 + end)[k]
            to = along(end * inner + mid * outer) if k == 2 else inner_peer
            ref = term(chunk, k)
            go(remote(ref, chunk.along.at[slot], chunk.send.at[41 + k], chunk.recv.at[41 + slot], to))

        def line_total(chunk):
            arrived(chunk, 0)

            if is_mid:
                arrived(chunk, 4)
                add_term(chunk, 0, (0, 4))

            if not is_mid:
                add_term(chunk, 0, (0,))

        def finish_z(chunk):
            arrived(chunk, 0)
            size = chunk.size // 2

            if is_mid:
                arrived(chunk, 4)

            for h in range(2):
                chunk.sum2[0, h].wait_recv()
                here = pl.ds(h * size, size)
                total = own_total(chunk, 0, h) + f32(chunk.along[0, :, here])

                if is_mid:
                    final[:, chunk.halves[h]] = (total + f32(chunk.along[4, :, here])).astype(bf16)

                if not is_mid:
                    final[:, chunk.halves[h]] = total.astype(bf16)

        def finish_x(chunk):
            for h in range(2):
                chunk.sum2[0, h].wait_recv()
                final[:, chunk.halves[h]] = own_total(chunk, 0, h).astype(bf16)

        graded = [0, 0]

        def hidden_step(step, _):
            cols = pl.ds(pl.multiple_of(step * 128, 128), 128)
            g = f32(gate[:, cols])
            u = f32(up[:, cols])
            value = g * jax.nn.sigmoid(g) * u
            hidden[:, cols] = value.astype(bf16)
            hidden_t[d, cols, :] = value.T.astype(bf16)
            return 0

        def forward(chunk, i):
            base = chunk.at + i * STEP
            cols = pl.ds(base, STEP)
            for b in range(ff // BLOCK):
                keep = jnp.concatenate(
                    [
                        jnp.full((16, BLOCK), f32(mask_ref[b, base // BLOCK + c])).astype(bf16)
                        for c in range(STEP // BLOCK)
                    ],
                    axis=1,
                )
                for r in range(BLOCK // 16):
                    rows = pl.ds(b * BLOCK + r * 16, 16)
                    weight[rows, cols] = weight[rows, cols] * keep
            part = jnp.dot(hidden[...], weight[:, cols], preferred_element_type=jnp.float32)
            partial[:, :, :, :, cols] = part.astype(bf16).reshape(partial.shape[:4] + (STEP,))

        def hidden_grad(chunk, part):
            begin, close = graded[part] == 0, graded[part] == len(CHUNKS) - 1
            graded[part] += 1
            wide = 512

            def step(i, _):
                rows = pl.ds(pl.multiple_of(i * wide, wide), wide)
                back = lax.dot_general(
                    cot[d, :, :, :, :, chunk.cols].reshape(tokens, chunk.size),
                    weight[rows, chunk.cols],
                    (((1,), (1,)), ((), ())),
                    preferred_element_type=jnp.float32,
                )
                if not begin:
                    back = back + acc[:, rows]
                if not close:
                    acc[:, rows] = back
                    return 0
                g = f32(gate[:, rows])
                u = f32(up[:, rows])
                s = jax.nn.sigmoid(g)
                gate_grad[:, rows] = (back * u * s * (1.0 + g * (1.0 - s))).astype(bf16)
                up_grad[:, rows] = (back * (g * s)).astype(bf16)
                return 0

            count = ff // wide // 2
            lax.fori_loop(part * count, (part + 1) * count, step, 0)

        def weight_half(chunk):
            size = chunk.size // 2
            base = pl.multiple_of(chunk.at + d * size, 256)
            cols = pl.ds(base, size)
            total = jnp.zeros((ff, size), jnp.float32)
            for core in range(2):
                total = total + jnp.dot(
                    hidden_t[core],
                    cot[core, :, :, :, :, cols].reshape(tokens, size),
                    preferred_element_type=jnp.float32,
                )
            for b in range(ff // BLOCK):
                for c in range(size // BLOCK):
                    keep = f32(mask_ref[b, chunk.at // BLOCK + d * (size // BLOCK) + c]) * scale
                    block = total[b * BLOCK : (b + 1) * BLOCK, c * BLOCK : (c + 1) * BLOCK]
                    at = pl.ds(pl.multiple_of(base + c * BLOCK, BLOCK), BLOCK)
                    weight_grad[pl.ds(b * BLOCK, BLOCK), at] = (block * keep).astype(bf16)
            chunk.half = go(
                remote(
                    weight_grad.at[:, cols], weight_grad.at[:, cols], chunk.send.at[46],
                    chunk.recv.at[46], core_peer,
                )
            )

        def do_loads():
            loads[0].wait()
            loads[1].wait()

        def do_hidden():
            lax.fori_loop(0, ff // 128, hidden_step, 0)
            hidden_core.start()

        def do_forward(c, i):
            if i == 0:
                weight_loads[c].wait()
            forward(chunks[c], i)

        def do_weight(c, _):
            for k in range(4):
                chunks[c].core[k].wait_recv()
            weight_half(chunks[c])

        actions = {
            "loads": do_loads,
            "hidden": do_hidden,
            "own": lambda: loads[2].wait(),
            "hcore": lambda: hidden_core.wait_recv(),
            "fwd": do_forward,
            "wg": do_weight,
            "hg": lambda c, part: hidden_grad(chunks[c], part),
            "gather": lambda c: gather_z(chunks[c]),
            "pass": lambda c, k: pass_z(chunks[c], k),
            "hop1": lambda c, k: hop1(chunks[c], k),
            "hop2": lambda c, k: hop2(chunks[c], k),
            "square": lambda c, k: square(chunks[c], k),
            "core": lambda c, k: to_core(chunks[c], k),
            "sum1": lambda c, k: sum1(chunks[c], k),
            "sum2": lambda c, k: sum2(chunks[c], k),
            "total": lambda c, k: square_total(chunks[c], k),
            "sumz": lambda c, k: sum_z(chunks[c], k),
            "line": lambda c: line_total(chunks[c]),
            "endz": lambda c: finish_z(chunks[c]),
            "endx": lambda c: finish_x(chunks[c]),
        }
        for name, *args in plan:
            actions[name](*args)

        for chunk in chunks:
            chunk.half.wait_recv()
        for copy in sent:
            copy.wait_send()

        hidden_core.wait_send()

    @pl.when(mid == 1)
    def _():
        run(True, MID_PLAN)

    @pl.when(end == 1)
    def _():
        run(False, END_PLAN)


def keep_in_hbm(array):
    return pltpu.with_memory_space_constraint(array, pltpu.HBM)


def chunk_scratch(rows, width):
    dma = pltpu.SemaphoreType.DMA
    bf16 = jnp.bfloat16
    scratch = []
    for (kind, _), (_, size) in zip(CHUNKS, chunk_columns(width)):
        levels = 4 if kind == "z" else 1
        held = (rows,) if kind == "z" else (2, 2, rows)
        scratch += [
            pltpu.VMEM((2, levels, 2, rows, size // 2), bf16),
            pltpu.VMEM((2, levels, rows, size // 2), bf16),
            pltpu.VMEM((5,) + held + (size,), bf16),
            dma((47,)),
            dma((47,)),
        ]
    return scratch


def fused(gate_pre, up_pre, down_weight, block_mask, out_grad):
    tokens, ff = gate_pre.shape
    rows, width = out_grad.shape
    scale = 1.0 / math.sqrt(tokens * 2)
    hbm = pl.BlockSpec(memory_space=pl.ANY)
    bf16 = jnp.bfloat16
    dma = pltpu.SemaphoreType.DMA
    results = pl.pallas_call(
        functools.partial(fused_kernel, scale),
        out_shape=(
            pltpu.VMEM((rows, width), bf16),
            pltpu.VMEM((tokens, ff), bf16),
            pltpu.VMEM((tokens, ff), bf16),
            pltpu.VMEM((ff, width), bf16),
        ),
        in_specs=[hbm, hbm, hbm, pl.BlockSpec(memory_space=pltpu.SMEM), hbm],
        out_specs=(pl.BlockSpec(memory_space=pltpu.VMEM),) * 4,
        scratch_shapes=[
            pltpu.VMEM((tokens, ff), bf16),
            pltpu.VMEM((tokens, ff), bf16),
            pltpu.VMEM((ff, width), bf16),
            pltpu.VMEM((2, 4, 2, 2, rows, width), bf16),
            pltpu.VMEM((tokens, ff), bf16),
            pltpu.VMEM((2, ff, tokens), bf16),
            pltpu.VMEM((4, 2, 2, rows, width), bf16),
            pltpu.VMEM((tokens, ff), jnp.float32),
            dma((3,)),
            dma((len(CHUNKS),)),
            dma((1,)),
            dma((1,)),
        ]
        + chunk_scratch(rows, width),
        compiler_params=pltpu.CompilerParams(
            collective_id=0, has_side_effects=True, vmem_limit_bytes=50 * 2**20
        ),
        cost_estimate=pl.CostEstimate(
            flops=8 * tokens * ff * width, bytes_accessed=40 * 2**20, transcendentals=2 * tokens * ff
        ),
    )(*(keep_in_hbm(a) for a in (gate_pre, up_pre, down_weight)), block_mask, keep_in_hbm(out_grad))
    return hand_on(results)


def hand_on_kernel(arrays, *refs):
    srcs, dsts, store_sem = refs[:arrays], refs[arrays : 2 * arrays], refs[2 * arrays]
    stores = [
        pltpu.make_async_copy(src, dst, store_sem.at[n])
        for n, (src, dst) in enumerate(zip(srcs, dsts))
    ]
    for store in stores:
        store.start()
    for store in stores:
        store.wait()


def hand_on(arrays):
    return pl.pallas_call(
        functools.partial(hand_on_kernel, len(arrays)),
        out_shape=tuple(jax.ShapeDtypeStruct(a.shape, a.dtype) for a in arrays),
        in_specs=[pl.BlockSpec(memory_space=pltpu.VMEM)] * len(arrays),
        out_specs=(pl.BlockSpec(memory_space=pl.ANY),) * len(arrays),
        scratch_shapes=[pltpu.SemaphoreType.DMA((len(arrays),))],
        compiler_params=pltpu.CompilerParams(vmem_limit_bytes=2 * 2**20),
    )(*(pltpu.with_memory_space_constraint(a, pltpu.VMEM) for a in arrays))


def local(gate_pre, up_pre, down_weight, block_mask, out_grad):
    blk_rows, blk_cols = block_mask.shape
    ff_local, width = down_weight.shape
    masked = (
        down_weight.reshape(blk_rows, 128, blk_cols, 128)
        * block_mask.astype(jnp.bfloat16)[:, None, :, None]
    ).reshape(ff_local, width)
    gate_val = gate_pre.astype(jnp.float32)
    up_val = up_pre.astype(jnp.float32)
    sigmoid_gate = jax.nn.sigmoid(gate_val)
    silu_gate = gate_val * sigmoid_gate
    hidden = (silu_gate * up_val).astype(jnp.bfloat16)
    layer_out = lax.psum_scatter(
        jnp.dot(hidden, masked, preferred_element_type=jnp.float32),
        "tensor",
        scatter_dimension=0,
        tiled=True,
    ).astype(jnp.bfloat16)
    cot_rows = lax.all_gather(out_grad, "tensor", axis=0, tiled=True)
    hidden_grad = lax.dot_general(
        cot_rows, masked, (((1,), (1,)), ((), ())), preferred_element_type=jnp.float32
    )
    gate_grad = (
        hidden_grad * up_val * sigmoid_gate * (1.0 + gate_val * (1.0 - sigmoid_gate))
    ).astype(jnp.bfloat16)
    up_grad = (hidden_grad * silu_gate).astype(jnp.bfloat16)
    tokens_all = out_grad.shape[0] * lax.axis_size("tensor") * lax.axis_size("dp")
    grad_scale = 1.0 / math.sqrt(tokens_all)
    partial_grad = (
        lax.dot_general(
            hidden, cot_rows, (((0,), (0,)), ((), ())), preferred_element_type=jnp.float32
        )
        * grad_scale
    )
    blocked = (
        partial_grad.reshape(blk_rows, 128, blk_cols, 128)
        * block_mask.astype(jnp.float32)[:, None, :, None]
    )
    summed = lax.psum(blocked.reshape(ff_local, width), "dp")
    weight_grad = summed.astype(jnp.bfloat16)
    return (layer_out, gate_grad, up_grad, weight_grad)


def solution(mesh):
    grouped = mesh.shape["dp"] == 2 and mesh.shape["tensor"] == 16
    return jax.shard_map(
        fused if grouped else local,
        mesh=mesh,
        in_specs=(
            P("dp", "tensor"),
            P("dp", "tensor"),
            P("tensor", None),
            P("tensor", None),
            P(("dp", "tensor"), None),
        ),
        out_specs=(
            P(("dp", "tensor"), None),
            P("dp", "tensor"),
            P("dp", "tensor"),
            P("tensor", None),
        ),
        check_vma=False,
    )
```

```python
import functools
import math

import jax
import jax.numpy as jnp
from jax import lax
from jax.experimental import pallas as pl
from jax.experimental.pallas import tpu as pltpu
from jax.sharding import PartitionSpec as P

BLOCK = 128
STEP = 512
CHUNKS = (("z", 2), ("z", 2), ("z", 1), ("x", 1), ("x", 2))
CHUNK_SCRATCH = 5


FORWARD = (2, 0, 1, 4, 3)
LATE = (3, )
MID_PLAN = (
    ("gather", 1), ("hop1", 4, 0), ("gather", 2), ("hop1", 3, 0), ("hop1", 1, 0), ("own",),
    ("hop1", 0, 0), ("hop1", 2, 0), ("gather", 0), ("hop2", 4, 0), ("pass", 1, 0), ("pass", 2, 1),
    ("pass", 1, 1), ("pass", 2, 0), ("loads",), ("hop2", 3, 0), ("hop1", 1, 1), ("pass", 0, 0),
    ("pass", 0, 1), ("hop1", 1, 2), ("hop2", 0, 0), ("pass", 2, 2), ("hop1", 0, 1),
    ("hop1", 2, 1), ("square", 4, 0), ("gather", 4), ("hop1", 2, 2), ("hidden",), ("hop2", 1, 1),
    ("square", 3, 0), ("pass", 1, 2), ("hop1", 1, 3), ("fwd", 2, 0), ("fwd", 0, 0),
    ("hop1", 2, 3), ("hop1", 0, 2), ("gather", 3), ("hop2", 0, 1), ("pass", 0, 2), ("hop2", 2, 1),
    ("fwd", 0, 1), ("sum1", 2, 3), ("fwd", 1, 0), ("sum1", 2, 1), ("fwd", 4, 0), ("pass", 4, 0),
    ("sum1", 0, 3), ("square", 1, 1), ("pass", 4, 1), ("fwd", 4, 1), ("hop2", 1, 2),
    ("core", 1, 1), ("hop1", 0, 3), ("sum2", 2, 1), ("hop2", 0, 2), ("fwd", 1, 1), ("pass", 3, 1),
    ("fwd", 3, 0), ("sumz", 3, 3), ("hop2", 1, 0), ("core", 4, 1), ("sum1", 2, 2), ("hop2", 1, 3),
    ("core", 3, 2), ("sum1", 1, 2), ("pass", 4, 2), ("hop2", 0, 3), ("sumz", 3, 1),
    ("pass", 3, 2), ("square", 0, 2), ("core", 4, 3), ("core", 4, 0), ("pass", 3, 0),
    ("core", 4, 2), ("sum1", 1, 1), ("square", 0, 0), ("hcore",), ("square", 1, 2),
    ("sum2", 2, 2), ("core", 0, 2), ("square", 1, 0), ("core", 0, 0), ("square", 1, 3),
    ("sum1", 0, 1), ("sum1", 1, 0), ("sum2", 2, 3), ("hg", 3, 0), ("sumz", 4, 3), ("hg", 4, 0),
    ("wg", 4, 0), ("hop2", 2, 0), ("square", 0, 3), ("core", 1, 0), ("core", 1, 2),
    ("core", 1, 3), ("hg", 3, 1), ("sum1", 1, 3), ("sumz", 3, 2), ("sum2", 1, 1),
    ("square", 0, 1), ("sum1", 0, 2), ("total", 2, 1), ("sum2", 0, 1), ("hg", 1, 0),
    ("sumz", 4, 1), ("hg", 4, 1), ("hop2", 2, 3), ("core", 0, 1), ("square", 2, 0),
    ("sum2", 0, 3), ("line", 3), ("total", 2, 3), ("sumz", 2, 3), ("sumz", 4, 2), ("core", 0, 3),
    ("hg", 0, 0), ("sum2", 1, 2), ("sum2", 1, 3), ("wg", 1, 0), ("square", 2, 1), ("hop2", 2, 2),
    ("sum1", 2, 0), ("core", 3, 1), ("sum2", 0, 2), ("wg", 0, 0), ("sum1", 3, 0), ("line", 4),
    ("total", 2, 2), ("total", 1, 3), ("core", 3, 3), ("sumz", 1, 3), ("total", 0, 3),
    ("sum1", 0, 0), ("square", 2, 3), ("core", 3, 0), ("core", 2, 3), ("sumz", 2, 2),
    ("sumz", 0, 3), ("core", 2, 1), ("sum1", 4, 0), ("square", 2, 2), ("core", 2, 2),
    ("core", 2, 0), ("total", 0, 1), ("total", 1, 1), ("hg", 2, 0), ("sum2", 2, 0),
    ("sumz", 1, 1), ("hg", 1, 1), ("sum2", 1, 0), ("total", 0, 2), ("total", 1, 2),
    ("sumz", 1, 2), ("wg", 3, 0), ("sum2", 3, 0), ("sum2", 0, 0), ("sumz", 0, 1), ("wg", 2, 0),
    ("sumz", 0, 2), ("sum2", 4, 0), ("sumz", 2, 1), ("hg", 2, 1), ("hg", 0, 1), ("endx", 3),
    ("endz", 0), ("endx", 4), ("endz", 1), ("endz", 2),
)
END_PLAN = (
    ("hop1", 3, 0), ("gather", 2), ("hop1", 4, 0), ("hop1", 1, 0), ("hop1", 2, 0), ("gather", 1),
    ("own",), ("gather", 0), ("hop1", 0, 0), ("loads",), ("hidden",), ("hop2", 4, 0),
    ("fwd", 3, 0), ("sumz", 3, 1), ("hop2", 3, 0), ("fwd", 2, 0), ("sum1", 2, 1), ("pass", 1, 0),
    ("pass", 2, 0), ("hop2", 1, 0), ("fwd", 4, 0), ("pass", 0, 0), ("fwd", 1, 0),
    ("square", 4, 0), ("gather", 4), ("hop1", 2, 1), ("sum1", 2, 3), ("square", 3, 0),
    ("gather", 3), ("hop1", 0, 1), ("hop1", 1, 1), ("pass", 2, 1), ("fwd", 0, 0), ("sum1", 2, 2),
    ("hop2", 2, 0), ("pass", 2, 2), ("hop1", 2, 3), ("hop2", 0, 0), ("pass", 0, 1),
    ("square", 1, 0), ("sumz", 3, 3), ("fwd", 1, 1), ("sum2", 2, 2), ("sum2", 2, 1),
    ("sum2", 2, 3), ("sum1", 1, 3), ("sumz", 3, 2), ("hop2", 2, 3), ("fwd", 4, 1), ("hop1", 2, 2),
    ("fwd", 0, 1), ("hop1", 0, 2), ("square", 0, 0), ("sumz", 4, 3), ("sum1", 0, 3),
    ("pass", 4, 0), ("sum1", 1, 2), ("sum1", 0, 2), ("hop2", 2, 1), ("hop2", 0, 1),
    ("pass", 0, 2), ("hop2", 0, 2), ("hop1", 0, 3), ("sumz", 4, 2), ("sum1", 0, 1),
    ("pass", 4, 1), ("sum2", 0, 3), ("square", 0, 2), ("square", 2, 3), ("sum2", 1, 2),
    ("hop2", 2, 2), ("total", 2, 3), ("core", 3, 0), ("pass", 1, 1), ("core", 4, 0),
    ("core", 2, 3), ("sumz", 2, 3), ("sum2", 1, 3), ("square", 0, 1), ("hop2", 0, 3),
    ("pass", 1, 2), ("square", 2, 1), ("hop2", 1, 1), ("core", 4, 1), ("total", 1, 2), ("hcore",),
    ("pass", 4, 2), ("hop1", 1, 2), ("core", 2, 1), ("sumz", 4, 1), ("hop1", 1, 3),
    ("sum2", 0, 2), ("hg", 4, 0), ("total", 1, 3), ("hg", 4, 1), ("pass", 3, 0), ("square", 2, 0),
    ("core", 4, 3), ("core", 4, 2), ("core", 0, 0), ("square", 2, 2), ("sum1", 1, 1),
    ("total", 2, 1), ("sum1", 2, 0), ("sumz", 1, 3), ("core", 2, 2), ("total", 0, 3),
    ("square", 0, 3), ("total", 2, 2), ("hg", 0, 0), ("hg", 0, 1), ("sum2", 0, 1), ("core", 2, 0),
    ("core", 0, 2), ("hop2", 1, 3), ("sumz", 0, 3), ("hop2", 1, 2), ("core", 0, 1),
    ("core", 0, 3), ("wg", 4, 0), ("hg", 2, 0), ("sumz", 1, 2), ("pass", 3, 1), ("sum2", 1, 1),
    ("square", 1, 1), ("wg", 0, 0), ("sum1", 0, 0), ("total", 0, 2), ("line", 3), ("sumz", 2, 1),
    ("sumz", 0, 2), ("total", 0, 1), ("sum1", 3, 0), ("core", 3, 1), ("sum1", 1, 0),
    ("sum2", 2, 0), ("pass", 3, 2), ("core", 3, 3), ("wg", 2, 0), ("core", 1, 0), ("hg", 3, 0),
    ("hg", 2, 1), ("square", 1, 2), ("sumz", 2, 2), ("total", 1, 1), ("square", 1, 3),
    ("core", 3, 2), ("core", 1, 2), ("sumz", 0, 1), ("core", 1, 1), ("sumz", 1, 1),
    ("core", 1, 3), ("line", 4), ("sum1", 4, 0), ("hg", 1, 0), ("sum2", 0, 0), ("wg", 3, 0),
    ("sum2", 3, 0), ("sum2", 1, 0), ("wg", 1, 0), ("sum2", 4, 0), ("endz", 2), ("hg", 1, 1),
    ("hg", 3, 1), ("endz", 0), ("endx", 3), ("endz", 1), ("endx", 4),
)


def remote(src, dst, send, recv, device):
    return pltpu.make_async_remote_copy(
        src_ref=src,
        dst_ref=dst,
        send_sem=send,
        recv_sem=recv,
        device_id=device,
        device_id_type=pl.DeviceIdType.MESH,
    )


def chunk_columns(width):
    unit = width // 8
    at, spans = 0, []
    for _, units in CHUNKS:
        spans.append((at, units * unit))
        at += units * unit
    return spans


def f32(value):
    return value.astype(jnp.float32)


def fused_kernel(
    scale,
    gate_hbm, up_hbm, weight_hbm, mask_ref, grad_hbm,
    final, gate_grad, up_grad, weight_grad, cot, hidden_t,
    gate, up, weight, hidden, partial, acc,
    in_sem, weight_sem, hidden_send, hidden_recv,
    *scratch,
):
    d = lax.axis_index("dp")
    t = lax.axis_index("tensor")
    x = t % 2
    y = (t // 2) % 2
    z = t // 4
    ff, width = weight.shape
    tokens = gate.shape[0]
    bf16 = jnp.bfloat16
    spans = chunk_columns(width)

    mid = ((z + 1) // 2) % 2
    end = 1 - mid
    is_mid = mid == 1
    inner = mid * (3 - z) + end * (1 + z // 3)
    outer = mid * (z - 1) * 3
    far = end * (3 - z) + mid * (2 - z) * 3
    blocks = (z, inner, end * (3 - inner) + mid * outer, far)

    def along(level):
        return {"tensor": level * 4 + y * 2 + x}

    x_peer = {"tensor": z * 4 + y * 2 + (1 - x)}
    y_peer = {"tensor": z * 4 + (1 - y) * 2 + x}
    core_peer = {"dp": 1 - d}
    inner_peer, outer_peer = along(inner), along(outer)

    loads = [
        pltpu.make_async_copy(gate_hbm, gate, in_sem.at[0]),
        pltpu.make_async_copy(up_hbm, up, in_sem.at[1]),
        pltpu.make_async_copy(grad_hbm, cot.at[d, z, y, x], in_sem.at[2]),
    ]
    weight_loads = {}
    for c, (at, size) in enumerate(spans):
        cols = pl.ds(at, size)
        weight_loads[c] = pltpu.make_async_copy(
            weight_hbm.at[:, cols], weight.at[:, cols], weight_sem.at[c]
        )
    for copy in loads:
        copy.start()
    for c in FORWARD:
        weight_loads[c].start()

    barrier = pltpu.get_barrier_semaphore()
    for peer in (x_peer, y_peer, core_peer, inner_peer):
        pl.semaphore_signal(barrier, inc=1, device_id=peer, device_id_type=pl.DeviceIdType.MESH)

    @pl.when(is_mid)
    def _():
        pl.semaphore_signal(
            barrier, inc=1, device_id=outer_peer, device_id_type=pl.DeviceIdType.MESH
        )

    pl.semaphore_wait(barrier, 4 + mid)

    def run(is_mid, plan):
        mid = int(is_mid)
        end = 1 - mid

        hidden_core = remote(
            hidden_t.at[d], hidden_t.at[d], hidden_send.at[0], hidden_recv.at[0], core_peer
        )
        sent = []

        def go(copy):
            copy.start()
            sent.append(copy)
            return copy

        class Chunk:
            pass

        def both_halves(chunk):
            return ((0, x_peer, y_peer, chunk.halves[0]), (1, y_peer, x_peer, chunk.halves[1]))

        chunks = []
        for c, (kind, _) in enumerate(CHUNKS):
            chunk = Chunk()
            at, size = spans[c]
            chunk.kind, chunk.at, chunk.size = kind, at, size
            chunk.cols = pl.ds(at, size)
            chunk.late = c in LATE
            chunk.halves = (pl.ds(at, size // 2), pl.ds(at + size // 2, size // 2))
            chunk.first, chunk.second, chunk.along, chunk.send, chunk.recv = scratch[
                CHUNK_SCRATCH * c : CHUNK_SCRATCH * (c + 1)
            ]
            chunk.hop1, chunk.hop2, chunk.core, chunk.sum1, chunk.sum2 = {}, {}, {}, {}, {}
            chunks.append(chunk)


        def piece(chunk, b):
            if chunk.kind == "z":
                return cot.at[d, b, y, x, :, chunk.cols]
            return cot.at[d, b, :, :, :, chunk.cols]

        def gather_z(chunk):
            own = piece(chunk, z)
            src = grad_hbm.at[:, chunk.cols] if chunk.kind == "z" else own
            go(remote(src, own, chunk.send.at[36], chunk.recv.at[36 + end], inner_peer))

            if is_mid:
                go(remote(src, own, chunk.send.at[37], chunk.recv.at[36], outer_peer))

        def pass_z(chunk, s):
            block = piece(chunk, blocks[s + 1])
            remote(block, block, chunk.send.at[36], chunk.recv.at[36 + s], inner_peer).wait_recv()
            if not is_mid:
                return
            to, slot = ((outer_peer, 1), (inner_peer, 2), (outer_peer, 2))[s]
            copy = remote(block, block, chunk.send.at[38 + s], chunk.recv.at[36 + slot], to)

            go(copy)

        def hop1(chunk, k):
            for h, near, _, half in both_halves(chunk):
                dst = cot.at[d, blocks[k], y, x, :, half]
                src = grad_hbm.at[:, half] if k == 0 else dst
                n = 2 * k + h
                chunk.hop1[k, h] = go(remote(src, dst, chunk.send.at[n], chunk.recv.at[n], near))

        def hop2(chunk, k):
            for h in range(2):
                chunk.hop1[k, h].wait_recv()
            for h, _, other, half in both_halves(chunk):
                ref = (cot.at[d, blocks[k], y, :, :, half], cot.at[d, blocks[k], :, x, :, half])[h]
                n = 8 + 2 * k + h
                chunk.hop2[k, h] = go(remote(ref, ref, chunk.send.at[n], chunk.recv.at[n], other))

        def square(chunk, k):
            for h in range(2):
                chunk.hop2[k, h].wait_recv()

        def to_core(chunk, k):
            size = chunk.size // 2
            cols = pl.ds(pl.multiple_of(chunk.at + (1 - d) * size, 256), size)
            if chunk.late:
                cols = chunk.cols
            ref = cot.at[d, blocks[k], :, :, :, cols]
            chunk.core[k] = go(
                remote(ref, ref, chunk.send.at[16 + k], chunk.recv.at[16 + k], core_peer)
            )

        def sum1(chunk, k):
            for h, near, _, half in both_halves(chunk):
                src = (
                    partial.at[blocks[k], :, 1 - x, :, half],
                    partial.at[blocks[k], 1 - y, :, :, half],
                )[h]
                n = 20 + 2 * k + h
                chunk.sum1[k, h] = go(
                    remote(src, chunk.first.at[h, k], chunk.send.at[n], chunk.recv.at[n], near)
                )

        def sum2(chunk, k):
            for h, _, other, half in both_halves(chunk):
                chunk.sum1[k, h].wait_recv()
                row, column, there = ((1 - y, x, 1 - y), (y, 1 - x, 1 - x))[h]
                total = f32(partial[blocks[k], row, column, :, half]) + f32(chunk.first[h, k, there])
                partial[blocks[k], row, column, :, half] = total.astype(bf16)
                n = 28 + 2 * k + h
                chunk.sum2[k, h] = go(
                    remote(
                        partial.at[blocks[k], row, column, :, half], chunk.second.at[h, k],
                        chunk.send.at[n], chunk.recv.at[n], other,
                    )
                )

        def own_total(chunk, k, h):
            mine = f32(partial[blocks[k], y, x, :, chunk.halves[h]])
            return mine + f32(chunk.first[h, k, (y, x)[h]]) + f32(chunk.second[h, k])

        def square_total(chunk, k):
            for h in range(2):
                chunk.sum2[k, h].wait_recv()
                partial[blocks[k], y, x, :, chunk.halves[h]] = own_total(chunk, k, h).astype(bf16)

        def term(chunk, k):
            if chunk.kind == "z":
                return partial.at[blocks[k], y, x, :, chunk.cols]
            return partial.at[blocks[k], :, :, :, chunk.cols]

        def arrived(chunk, slot):
            ref = chunk.along.at[slot]
            remote(ref, ref, chunk.send.at[41], chunk.recv.at[41 + slot], inner_peer).wait_recv()

        def add_term(chunk, k, slots):
            if chunk.kind == "z":
                total = f32(partial[blocks[k], y, x, :, chunk.cols])
                for slot in slots:
                    total = total + f32(chunk.along[slot])
                partial[blocks[k], y, x, :, chunk.cols] = total.astype(bf16)
                return

            wide = 256

            def step(i, _):
                here = pl.ds(pl.multiple_of(i * wide, wide), wide)
                cols = pl.ds(pl.multiple_of(chunk.at + i * wide, wide), wide)
                total = f32(partial[blocks[k], :, :, :, cols])
                for slot in slots:
                    total = total + f32(chunk.along[slot, :, :, :, here])
                partial[blocks[k], :, :, :, cols] = total.astype(bf16)
                return 0

            lax.fori_loop(0, chunk.size // wide, step, 0)

        def sum_z(chunk, k):
            if is_mid:
                arrived(chunk, k)
                add_term(chunk, k, (k,))

            slot = (None, 4 * mid, end, 2 + end)[k]
            to = along(end * inner + mid * outer) if k == 2 else inner_peer
            ref = term(chunk, k)
            go(remote(ref, chunk.along.at[slot], chunk.send.at[41 + k], chunk.recv.at[41 + slot], to))

        def line_total(chunk):
            arrived(chunk, 0)

            if is_mid:
                arrived(chunk, 4)
                add_term(chunk, 0, (0, 4))

            if not is_mid:
                add_term(chunk, 0, (0,))

        def finish_z(chunk):
            arrived(chunk, 0)
            size = chunk.size // 2

            if is_mid:
                arrived(chunk, 4)

            for h in range(2):
                chunk.sum2[0, h].wait_recv()
                here = pl.ds(h * size, size)
                total = own_total(chunk, 0, h) + f32(chunk.along[0, :, here])

                if is_mid:
                    final[:, chunk.halves[h]] = (total + f32(chunk.along[4, :, here])).astype(bf16)

                if not is_mid:
                    final[:, chunk.halves[h]] = total.astype(bf16)

        def finish_x(chunk):
            for h in range(2):
                chunk.sum2[0, h].wait_recv()
                final[:, chunk.halves[h]] = own_total(chunk, 0, h).astype(bf16)

        graded = [0, 0]

        def hidden_step(step, _):
            cols = pl.ds(pl.multiple_of(step * 128, 128), 128)
            g = f32(gate[:, cols])
            u = f32(up[:, cols])
            value = g * jax.nn.sigmoid(g) * u
            hidden[:, cols] = value.astype(bf16)
            hidden_t[d, cols, :] = value.T.astype(bf16)
            return 0

        def forward(chunk, i):
            base = chunk.at + i * STEP
            cols = pl.ds(base, STEP)
            for b in range(ff // BLOCK):
                keep = jnp.concatenate(
                    [
                        jnp.full((16, BLOCK), f32(mask_ref[b, base // BLOCK + c])).astype(bf16)
                        for c in range(STEP // BLOCK)
                    ],
                    axis=1,
                )
                for r in range(BLOCK // 16):
                    rows = pl.ds(b * BLOCK + r * 16, 16)
                    weight[rows, cols] = weight[rows, cols] * keep
            part = jnp.dot(hidden[...], weight[:, cols], preferred_element_type=jnp.float32)
            partial[:, :, :, :, cols] = part.astype(bf16).reshape(partial.shape[:4] + (STEP,))

        def hidden_grad(chunk, part):
            begin, close = graded[part] == 0, graded[part] == len(CHUNKS) - 1
            graded[part] += 1
            wide = 512

            def step(i, _):
                rows = pl.ds(pl.multiple_of(i * wide, wide), wide)
                back = lax.dot_general(
                    cot[d, :, :, :, :, chunk.cols].reshape(tokens, chunk.size),
                    weight[rows, chunk.cols],
                    (((1,), (1,)), ((), ())),
                    preferred_element_type=jnp.float32,
                )
                if not begin:
                    back = back + acc[:, rows]
                if not close:
                    acc[:, rows] = back
                    return 0
                g = f32(gate[:, rows])
                u = f32(up[:, rows])
                s = jax.nn.sigmoid(g)
                gate_grad[:, rows] = (back * u * s * (1.0 + g * (1.0 - s))).astype(bf16)
                up_grad[:, rows] = (back * (g * s)).astype(bf16)
                return 0

            count = ff // wide // 2
            lax.fori_loop(part * count, (part + 1) * count, step, 0)

        def weight_half(chunk):
            size = chunk.size // 2
            base = pl.multiple_of(chunk.at + d * size, 256)
            cols = pl.ds(base, size)
            total = jnp.zeros((ff, size), jnp.float32)
            for core in range(2):
                total = total + jnp.dot(
                    hidden_t[core],
                    cot[core, :, :, :, :, cols].reshape(tokens, size),
                    preferred_element_type=jnp.float32,
                )
            for b in range(ff // BLOCK):
                for c in range(size // BLOCK):
                    keep = f32(mask_ref[b, chunk.at // BLOCK + d * (size // BLOCK) + c]) * scale
                    block = total[b * BLOCK : (b + 1) * BLOCK, c * BLOCK : (c + 1) * BLOCK]
                    at = pl.ds(pl.multiple_of(base + c * BLOCK, BLOCK), BLOCK)
                    weight_grad[pl.ds(b * BLOCK, BLOCK), at] = (block * keep).astype(bf16)
            chunk.half = go(
                remote(
                    weight_grad.at[:, cols], weight_grad.at[:, cols], chunk.send.at[46],
                    chunk.recv.at[46], core_peer,
                )
            )

        def do_loads():
            loads[0].wait()
            loads[1].wait()

        def do_hidden():
            lax.fori_loop(0, ff // 128, hidden_step, 0)
            hidden_core.start()

        def do_forward(c, i):
            if i == 0:
                weight_loads[c].wait()
            forward(chunks[c], i)

        def do_weight(c, _):
            for k in range(4):
                chunks[c].core[k].wait_recv()
            if not chunks[c].late:
                weight_half(chunks[c])

        actions = {
            "loads": do_loads,
            "hidden": do_hidden,
            "own": lambda: loads[2].wait(),
            "hcore": lambda: hidden_core.wait_recv(),
            "fwd": do_forward,
            "wg": do_weight,
            "hg": lambda c, part: hidden_grad(chunks[c], part),
            "gather": lambda c: gather_z(chunks[c]),
            "pass": lambda c, k: pass_z(chunks[c], k),
            "hop1": lambda c, k: hop1(chunks[c], k),
            "hop2": lambda c, k: hop2(chunks[c], k),
            "square": lambda c, k: square(chunks[c], k),
            "core": lambda c, k: to_core(chunks[c], k),
            "sum1": lambda c, k: sum1(chunks[c], k),
            "sum2": lambda c, k: sum2(chunks[c], k),
            "total": lambda c, k: square_total(chunks[c], k),
            "sumz": lambda c, k: sum_z(chunks[c], k),
            "line": lambda c: line_total(chunks[c]),
            "endz": lambda c: finish_z(chunks[c]),
            "endx": lambda c: finish_x(chunks[c]),
        }
        for name, *args in plan:
            actions[name](*args)

        for chunk in chunks:
            if not chunk.late:
                chunk.half.wait_recv()
        for copy in sent:
            copy.wait_send()

        hidden_core.wait_send()

    @pl.when(mid == 1)
    def _():
        run(True, MID_PLAN)

    @pl.when(end == 1)
    def _():
        run(False, END_PLAN)


def keep_in_hbm(array):
    return pltpu.with_memory_space_constraint(array, pltpu.HBM)


def chunk_scratch(rows, width):
    dma = pltpu.SemaphoreType.DMA
    bf16 = jnp.bfloat16
    scratch = []
    for (kind, _), (_, size) in zip(CHUNKS, chunk_columns(width)):
        levels = 4 if kind == "z" else 1
        held = (rows,) if kind == "z" else (2, 2, rows)
        scratch += [
            pltpu.VMEM((2, levels, 2, rows, size // 2), bf16),
            pltpu.VMEM((2, levels, rows, size // 2), bf16),
            pltpu.VMEM((5,) + held + (size,), bf16),
            dma((47,)),
            dma((47,)),
        ]
    return scratch


def fused(gate_pre, up_pre, down_weight, block_mask, out_grad):
    tokens, ff = gate_pre.shape
    rows, width = out_grad.shape
    scale = 1.0 / math.sqrt(tokens * 2)
    hbm = pl.BlockSpec(memory_space=pl.ANY)
    bf16 = jnp.bfloat16
    dma = pltpu.SemaphoreType.DMA
    results = pl.pallas_call(
        functools.partial(fused_kernel, scale),
        out_shape=(
            pltpu.VMEM((rows, width), bf16),
            pltpu.VMEM((tokens, ff), bf16),
            pltpu.VMEM((tokens, ff), bf16),
            pltpu.VMEM((ff, width), bf16),
            pltpu.VMEM((2, 4, 2, 2, rows, width), bf16),
            pltpu.VMEM((2, ff, tokens), bf16),
        ),
        in_specs=[hbm, hbm, hbm, pl.BlockSpec(memory_space=pltpu.SMEM), hbm],
        out_specs=(pl.BlockSpec(memory_space=pltpu.VMEM),) * 6,
        scratch_shapes=[
            pltpu.VMEM((tokens, ff), bf16),
            pltpu.VMEM((tokens, ff), bf16),
            pltpu.VMEM((ff, width), bf16),
            pltpu.VMEM((tokens, ff), bf16),
            pltpu.VMEM((4, 2, 2, rows, width), bf16),
            pltpu.VMEM((tokens, ff), jnp.float32),
            dma((3,)),
            dma((len(CHUNKS),)),
            dma((1,)),
            dma((1,)),
        ]
        + chunk_scratch(rows, width),
        compiler_params=pltpu.CompilerParams(
            collective_id=0, has_side_effects=True, vmem_limit_bytes=38 * 2**20
        ),
        cost_estimate=pl.CostEstimate(
            flops=8 * tokens * ff * width, bytes_accessed=40 * 2**20, transcendentals=2 * tokens * ff
        ),
    )(*(keep_in_hbm(a) for a in (gate_pre, up_pre, down_weight, block_mask, out_grad)))
    return hand_on(scale, block_mask, *results)


def hand_on_kernel(
    scale, mask_hbm, final, gate_grad, up_grad, weight_grad, cot, hidden_t,
    final_hbm, gate_grad_hbm, up_grad_hbm, weight_grad_hbm, mask_ref, tile, store_sem, mask_sem,
):
    ff, width = weight_grad.shape
    tokens = hidden_t.shape[2]
    spans = chunk_columns(width)
    stores = []

    def store(src, dst):
        copy = pltpu.make_async_copy(src, dst, store_sem.at[len(stores)])
        copy.start()
        stores.append(copy)

    mask_load = pltpu.make_async_copy(mask_hbm, mask_ref, mask_sem.at[0])
    mask_load.start()
    runs = []
    for c, (at, size) in enumerate(spans):
        if c in LATE:
            continue
        if runs and sum(runs[-1]) == at:
            at, size = runs[-1][0], runs[-1][1] + size
            runs.pop()
        runs.append((at, size))
    for at, size in runs:
        store(weight_grad.at[:, pl.ds(at, size)], weight_grad_hbm.at[:, pl.ds(at, size)])
    store(gate_grad, gate_grad_hbm)
    store(up_grad, up_grad_hbm)
    store(final, final_hbm)
    wide = 512
    put = 0
    mask_load.wait()
    for c in LATE:
        at, size = spans[c]
        for first in range(at, at + size, wide):
            cols = pl.ds(first, wide)
            total = jnp.zeros((ff, wide), jnp.float32)
            for core in range(2):
                total = total + jnp.dot(
                    hidden_t[core],
                    cot[core, :, :, :, :, cols].reshape(tokens, wide),
                    preferred_element_type=jnp.float32,
                )
            for b in range(ff // BLOCK):
                for n in range(wide // BLOCK):
                    keep = f32(mask_ref[b, first // BLOCK + n]) * scale
                    block = total[b * BLOCK : (b + 1) * BLOCK, n * BLOCK : (n + 1) * BLOCK]
                    tile[pl.ds(b * BLOCK, BLOCK), pl.ds(put + n * BLOCK, BLOCK)] = (
                        block * keep
                    ).astype(jnp.bfloat16)
            store(tile.at[:, pl.ds(put, wide)], weight_grad_hbm.at[:, cols])
            put += wide
    for copy in stores:
        copy.wait()


def hand_on(scale, block_mask, *arrays):
    ff, width = arrays[3].shape
    late = sum(chunk_columns(width)[c][1] for c in LATE)
    held = pl.BlockSpec(memory_space=pltpu.VMEM)
    return pl.pallas_call(
        functools.partial(hand_on_kernel, scale),
        out_shape=tuple(jax.ShapeDtypeStruct(a.shape, a.dtype) for a in arrays[:4]),
        in_specs=[pl.BlockSpec(memory_space=pl.ANY)] + [held] * len(arrays),
        out_specs=(pl.BlockSpec(memory_space=pl.ANY),) * 4,
        scratch_shapes=[
            pltpu.SMEM(block_mask.shape, jnp.int32),
            pltpu.VMEM((ff, late), jnp.bfloat16),
            pltpu.SemaphoreType.DMA((len(CHUNKS) + 3 + late // 512,)),
            pltpu.SemaphoreType.DMA((1,)),
        ],
        compiler_params=pltpu.CompilerParams(vmem_limit_bytes=12 * 2**20),
    )(keep_in_hbm(block_mask), *(pltpu.with_memory_space_constraint(a, pltpu.VMEM) for a in arrays))


def local(gate_pre, up_pre, down_weight, block_mask, out_grad):
    blk_rows, blk_cols = block_mask.shape
    ff_local, width = down_weight.shape
    masked = (
        down_weight.reshape(blk_rows, 128, blk_cols, 128)
        * block_mask.astype(jnp.bfloat16)[:, None, :, None]
    ).reshape(ff_local, width)
    gate_val = gate_pre.astype(jnp.float32)
    up_val = up_pre.astype(jnp.float32)
    sigmoid_gate = jax.nn.sigmoid(gate_val)
    silu_gate = gate_val * sigmoid_gate
    hidden = (silu_gate * up_val).astype(jnp.bfloat16)
    layer_out = lax.psum_scatter(
        jnp.dot(hidden, masked, preferred_element_type=jnp.float32),
        "tensor",
        scatter_dimension=0,
        tiled=True,
    ).astype(jnp.bfloat16)
    cot_rows = lax.all_gather(out_grad, "tensor", axis=0, tiled=True)
    hidden_grad = lax.dot_general(
        cot_rows, masked, (((1,), (1,)), ((), ())), preferred_element_type=jnp.float32
    )
    gate_grad = (
        hidden_grad * up_val * sigmoid_gate * (1.0 + gate_val * (1.0 - sigmoid_gate))
    ).astype(jnp.bfloat16)
    up_grad = (hidden_grad * silu_gate).astype(jnp.bfloat16)
    tokens_all = out_grad.shape[0] * lax.axis_size("tensor") * lax.axis_size("dp")
    grad_scale = 1.0 / math.sqrt(tokens_all)
    partial_grad = (
        lax.dot_general(
            hidden, cot_rows, (((0,), (0,)), ((), ())), preferred_element_type=jnp.float32
        )
        * grad_scale
    )
    blocked = (
        partial_grad.reshape(blk_rows, 128, blk_cols, 128)
        * block_mask.astype(jnp.float32)[:, None, :, None]
    )
    summed = lax.psum(blocked.reshape(ff_local, width), "dp")
    weight_grad = summed.astype(jnp.bfloat16)
    return (layer_out, gate_grad, up_grad, weight_grad)


def solution(mesh):
    grouped = mesh.shape["dp"] == 2 and mesh.shape["tensor"] == 16
    return jax.shard_map(
        fused if grouped else local,
        mesh=mesh,
        in_specs=(
            P("dp", "tensor"),
            P("dp", "tensor"),
            P("tensor", None),
            P("tensor", None),
            P(("dp", "tensor"), None),
        ),
        out_specs=(
            P(("dp", "tensor"), None),
            P("dp", "tensor"),
            P("dp", "tensor"),
            P("tensor", None),
        ),
        check_vma=False,
    )
```

```python
import functools
import math

import jax
import jax.numpy as jnp
from jax import lax
from jax.experimental import pallas as pl
from jax.experimental.pallas import tpu as pltpu
from jax.sharding import PartitionSpec as P

BLOCK = 128
STEP = 512
CHUNKS = (("z", 2), ("z", 2), ("z", 1), ("x", 1), ("x", 2))
CHUNK_SCRATCH = 5


FORWARD = (2, 0, 1, 4, 3)
LATE = (3, )
MID_PLAN = (
    ("gather", 1), ("hop1", 4, 0), ("gather", 2), ("hop1", 3, 0), ("hop1", 1, 0), ("own",),
    ("hop1", 0, 0), ("hop1", 2, 0), ("gather", 0), ("hop2", 4, 0), ("pass", 1, 0), ("pass", 2, 1),
    ("pass", 1, 1), ("pass", 2, 0), ("loads",), ("hop2", 3, 0), ("hop1", 1, 1), ("pass", 0, 0),
    ("pass", 0, 1), ("hop1", 1, 2), ("hop2", 0, 0), ("pass", 2, 2), ("hop1", 0, 1),
    ("hop1", 2, 1), ("square", 4, 0), ("gather", 4), ("hop1", 2, 2), ("hidden",), ("hop2", 1, 1),
    ("square", 3, 0), ("pass", 1, 2), ("hop1", 1, 3), ("fwd", 2, 0), ("fwd", 0, 0),
    ("hop1", 2, 3), ("hop1", 0, 2), ("gather", 3), ("hop2", 0, 1), ("pass", 0, 2), ("hop2", 2, 1),
    ("fwd", 0, 1), ("sum1", 2, 3), ("fwd", 1, 0), ("sum1", 2, 1), ("fwd", 4, 0), ("pass", 4, 0),
    ("sum1", 0, 3), ("square", 1, 1), ("pass", 4, 1), ("fwd", 4, 1), ("hop2", 1, 2),
    ("core", 1, 1), ("hop1", 0, 3), ("sum2", 2, 1), ("hop2", 0, 2), ("fwd", 1, 1), ("pass", 3, 1),
    ("fwd", 3, 0), ("sumz", 3, 3), ("hop2", 1, 0), ("core", 4, 1), ("sum1", 2, 2), ("hop2", 1, 3),
    ("core", 3, 2), ("sum1", 1, 2), ("pass", 4, 2), ("hop2", 0, 3), ("sumz", 3, 1),
    ("pass", 3, 2), ("square", 0, 2), ("core", 4, 3), ("core", 4, 0), ("pass", 3, 0),
    ("core", 4, 2), ("sum1", 1, 1), ("square", 0, 0), ("hcore",), ("square", 1, 2),
    ("sum2", 2, 2), ("core", 0, 2), ("square", 1, 0), ("core", 0, 0), ("square", 1, 3),
    ("sum1", 0, 1), ("sum1", 1, 0), ("sum2", 2, 3), ("hg", 3, 0), ("sumz", 4, 3), ("hg", 4, 0),
    ("wg", 4, 0), ("hop2", 2, 0), ("square", 0, 3), ("core", 1, 0), ("core", 1, 2),
    ("core", 1, 3), ("hg", 3, 1), ("sum1", 1, 3), ("sumz", 3, 2), ("sum2", 1, 1),
    ("square", 0, 1), ("sum1", 0, 2), ("total", 2, 1), ("sum2", 0, 1), ("hg", 1, 0),
    ("sumz", 4, 1), ("hg", 4, 1), ("hop2", 2, 3), ("core", 0, 1), ("square", 2, 0),
    ("sum2", 0, 3), ("line", 3), ("total", 2, 3), ("sumz", 2, 3), ("sumz", 4, 2), ("core", 0, 3),
    ("hg", 0, 0), ("sum2", 1, 2), ("sum2", 1, 3), ("wg", 1, 0), ("square", 2, 1), ("hop2", 2, 2),
    ("sum1", 2, 0), ("core", 3, 1), ("sum2", 0, 2), ("wg", 0, 0), ("sum1", 3, 0), ("line", 4),
    ("total", 2, 2), ("total", 1, 3), ("core", 3, 3), ("sumz", 1, 3), ("total", 0, 3),
    ("sum1", 0, 0), ("square", 2, 3), ("core", 3, 0), ("core", 2, 3), ("sumz", 2, 2),
    ("sumz", 0, 3), ("core", 2, 1), ("sum1", 4, 0), ("square", 2, 2), ("core", 2, 2),
    ("core", 2, 0), ("total", 0, 1), ("total", 1, 1), ("hg", 2, 0), ("sum2", 2, 0),
    ("sumz", 1, 1), ("hg", 1, 1), ("sum2", 1, 0), ("total", 0, 2), ("total", 1, 2),
    ("sumz", 1, 2), ("wg", 3, 0), ("sum2", 3, 0), ("sum2", 0, 0), ("sumz", 0, 1), ("wg", 2, 0),
    ("sumz", 0, 2), ("sum2", 4, 0), ("sumz", 2, 1), ("hg", 2, 1), ("hg", 0, 1), ("endx", 3),
    ("endz", 0), ("endx", 4), ("endz", 1), ("endz", 2),
)
END_PLAN = (
    ("hop1", 3, 0), ("gather", 2), ("hop1", 4, 0), ("hop1", 1, 0), ("hop1", 2, 0), ("gather", 1),
    ("own",), ("gather", 0), ("hop1", 0, 0), ("loads",), ("hidden",), ("hop2", 4, 0),
    ("fwd", 3, 0), ("sumz", 3, 1), ("hop2", 3, 0), ("fwd", 2, 0), ("sum1", 2, 1), ("pass", 1, 0),
    ("pass", 2, 0), ("hop2", 1, 0), ("fwd", 4, 0), ("pass", 0, 0), ("fwd", 1, 0),
    ("square", 4, 0), ("gather", 4), ("hop1", 2, 1), ("sum1", 2, 3), ("square", 3, 0),
    ("gather", 3), ("hop1", 0, 1), ("hop1", 1, 1), ("pass", 2, 1), ("fwd", 0, 0), ("sum1", 2, 2),
    ("hop2", 2, 0), ("pass", 2, 2), ("hop1", 2, 3), ("hop2", 0, 0), ("pass", 0, 1),
    ("square", 1, 0), ("sumz", 3, 3), ("fwd", 1, 1), ("sum2", 2, 2), ("sum2", 2, 1),
    ("sum2", 2, 3), ("sum1", 1, 3), ("sumz", 3, 2), ("hop2", 2, 3), ("fwd", 4, 1), ("hop1", 2, 2),
    ("fwd", 0, 1), ("hop1", 0, 2), ("square", 0, 0), ("sumz", 4, 3), ("sum1", 0, 3),
    ("pass", 4, 0), ("sum1", 1, 2), ("sum1", 0, 2), ("hop2", 2, 1), ("hop2", 0, 1),
    ("pass", 0, 2), ("hop2", 0, 2), ("hop1", 0, 3), ("sumz", 4, 2), ("sum1", 0, 1),
    ("pass", 4, 1), ("sum2", 0, 3), ("square", 0, 2), ("square", 2, 3), ("sum2", 1, 2),
    ("hop2", 2, 2), ("total", 2, 3), ("core", 3, 0), ("pass", 1, 1), ("core", 4, 0),
    ("core", 2, 3), ("sumz", 2, 3), ("sum2", 1, 3), ("square", 0, 1), ("hop2", 0, 3),
    ("pass", 1, 2), ("square", 2, 1), ("hop2", 1, 1), ("core", 4, 1), ("total", 1, 2), ("hcore",),
    ("pass", 4, 2), ("hop1", 1, 2), ("core", 2, 1), ("sumz", 4, 1), ("hop1", 1, 3),
    ("sum2", 0, 2), ("hg", 4, 0), ("total", 1, 3), ("hg", 4, 1), ("pass", 3, 0), ("square", 2, 0),
    ("core", 4, 3), ("core", 4, 2), ("core", 0, 0), ("square", 2, 2), ("sum1", 1, 1),
    ("total", 2, 1), ("sum1", 2, 0), ("sumz", 1, 3), ("core", 2, 2), ("total", 0, 3),
    ("square", 0, 3), ("total", 2, 2), ("hg", 0, 0), ("hg", 0, 1), ("sum2", 0, 1), ("core", 2, 0),
    ("core", 0, 2), ("hop2", 1, 3), ("sumz", 0, 3), ("hop2", 1, 2), ("core", 0, 1),
    ("core", 0, 3), ("wg", 4, 0), ("hg", 2, 0), ("sumz", 1, 2), ("pass", 3, 1), ("sum2", 1, 1),
    ("square", 1, 1), ("wg", 0, 0), ("sum1", 0, 0), ("total", 0, 2), ("line", 3), ("sumz", 2, 1),
    ("sumz", 0, 2), ("total", 0, 1), ("sum1", 3, 0), ("core", 3, 1), ("sum1", 1, 0),
    ("sum2", 2, 0), ("pass", 3, 2), ("core", 3, 3), ("wg", 2, 0), ("core", 1, 0), ("hg", 3, 0),
    ("hg", 2, 1), ("square", 1, 2), ("sumz", 2, 2), ("total", 1, 1), ("square", 1, 3),
    ("core", 3, 2), ("core", 1, 2), ("sumz", 0, 1), ("core", 1, 1), ("sumz", 1, 1),
    ("core", 1, 3), ("line", 4), ("sum1", 4, 0), ("hg", 1, 0), ("sum2", 0, 0), ("wg", 3, 0),
    ("sum2", 3, 0), ("sum2", 1, 0), ("wg", 1, 0), ("sum2", 4, 0), ("endz", 2), ("hg", 1, 1),
    ("hg", 3, 1), ("endz", 0), ("endx", 3), ("endz", 1), ("endx", 4),
)


def remote(src, dst, send, recv, device):
    return pltpu.make_async_remote_copy(
        src_ref=src,
        dst_ref=dst,
        send_sem=send,
        recv_sem=recv,
        device_id=device,
        device_id_type=pl.DeviceIdType.MESH,
    )


def chunk_columns(width):
    unit = width // 8
    at, spans = 0, []
    for _, units in CHUNKS:
        spans.append((at, units * unit))
        at += units * unit
    return spans


def f32(value):
    return value.astype(jnp.float32)


def fused_kernel(
    scale,
    gate_hbm, up_hbm, weight_hbm, mask_ref, grad_hbm,
    final, gate_grad, up_grad, weight_grad, cot, hidden_t,
    gate, up, weight, hidden, partial, acc,
    in_sem, weight_sem, hidden_send, hidden_recv,
    *scratch,
):
    d = lax.axis_index("dp")
    t = lax.axis_index("tensor")
    x = t % 2
    y = (t // 2) % 2
    z = t // 4
    ff, width = weight.shape
    tokens = gate.shape[0]
    bf16 = jnp.bfloat16
    spans = chunk_columns(width)

    mid = ((z + 1) // 2) % 2
    end = 1 - mid
    is_mid = mid == 1
    inner = mid * (3 - z) + end * (1 + z // 3)
    outer = mid * (z - 1) * 3
    far = end * (3 - z) + mid * (2 - z) * 3
    blocks = (z, inner, end * (3 - inner) + mid * outer, far)

    def along(level):
        return {"tensor": level * 4 + y * 2 + x}

    x_peer = {"tensor": z * 4 + y * 2 + (1 - x)}
    y_peer = {"tensor": z * 4 + (1 - y) * 2 + x}
    core_peer = {"dp": 1 - d}
    inner_peer, outer_peer = along(inner), along(outer)

    loads = [
        pltpu.make_async_copy(gate_hbm, gate, in_sem.at[0]),
        pltpu.make_async_copy(up_hbm, up, in_sem.at[1]),
        pltpu.make_async_copy(grad_hbm, cot.at[d, z, y, x], in_sem.at[2]),
    ]
    weight_loads = {}
    for c, (at, size) in enumerate(spans):
        cols = pl.ds(at, size)
        weight_loads[c] = pltpu.make_async_copy(
            weight_hbm.at[:, cols], weight.at[:, cols], weight_sem.at[c]
        )
    barrier = pltpu.get_barrier_semaphore()
    for peer in (x_peer, y_peer, core_peer, inner_peer):
        pl.semaphore_signal(barrier, inc=1, device_id=peer, device_id_type=pl.DeviceIdType.MESH)

    @pl.when(is_mid)
    def _():
        pl.semaphore_signal(
            barrier, inc=1, device_id=outer_peer, device_id_type=pl.DeviceIdType.MESH
        )

    for copy in loads:
        copy.start()
    for c in FORWARD:
        weight_loads[c].start()

    pl.semaphore_wait(barrier, 4 + mid)

    def run(is_mid, plan):
        mid = int(is_mid)
        end = 1 - mid

        hidden_core = remote(
            hidden_t.at[d], hidden_t.at[d], hidden_send.at[0], hidden_recv.at[0], core_peer
        )
        sent = []

        def go(copy):
            copy.start()
            sent.append(copy)
            return copy

        class Chunk:
            pass

        def both_halves(chunk):
            return ((0, x_peer, y_peer, chunk.halves[0]), (1, y_peer, x_peer, chunk.halves[1]))

        chunks = []
        for c, (kind, _) in enumerate(CHUNKS):
            chunk = Chunk()
            at, size = spans[c]
            chunk.kind, chunk.at, chunk.size = kind, at, size
            chunk.cols = pl.ds(at, size)
            chunk.late = c in LATE
            chunk.halves = (pl.ds(at, size // 2), pl.ds(at + size // 2, size // 2))
            chunk.first, chunk.second, chunk.along, chunk.send, chunk.recv = scratch[
                CHUNK_SCRATCH * c : CHUNK_SCRATCH * (c + 1)
            ]
            chunk.hop1, chunk.hop2, chunk.core, chunk.sum1, chunk.sum2 = {}, {}, {}, {}, {}
            chunks.append(chunk)


        def piece(chunk, b):
            if chunk.kind == "z":
                return cot.at[d, b, y, x, :, chunk.cols]
            return cot.at[d, b, :, :, :, chunk.cols]

        def gather_z(chunk):
            own = piece(chunk, z)
            src = grad_hbm.at[:, chunk.cols] if chunk.kind == "z" else own
            go(remote(src, own, chunk.send.at[36], chunk.recv.at[36 + end], inner_peer))

            if is_mid:
                go(remote(src, own, chunk.send.at[37], chunk.recv.at[36], outer_peer))

        def pass_z(chunk, s):
            block = piece(chunk, blocks[s + 1])
            remote(block, block, chunk.send.at[36], chunk.recv.at[36 + s], inner_peer).wait_recv()
            if not is_mid:
                return
            to, slot = ((outer_peer, 1), (inner_peer, 2), (outer_peer, 2))[s]
            copy = remote(block, block, chunk.send.at[38 + s], chunk.recv.at[36 + slot], to)

            go(copy)

        def hop1(chunk, k):
            for h, near, _, half in both_halves(chunk):
                dst = cot.at[d, blocks[k], y, x, :, half]
                src = grad_hbm.at[:, half] if k == 0 else dst
                n = 2 * k + h
                chunk.hop1[k, h] = go(remote(src, dst, chunk.send.at[n], chunk.recv.at[n], near))

        def hop2(chunk, k):
            for h in range(2):
                chunk.hop1[k, h].wait_recv()
            for h, _, other, half in both_halves(chunk):
                ref = (cot.at[d, blocks[k], y, :, :, half], cot.at[d, blocks[k], :, x, :, half])[h]
                n = 8 + 2 * k + h
                chunk.hop2[k, h] = go(remote(ref, ref, chunk.send.at[n], chunk.recv.at[n], other))

        def square(chunk, k):
            for h in range(2):
                chunk.hop2[k, h].wait_recv()

        def to_core(chunk, k):
            size = chunk.size // 2
            cols = pl.ds(pl.multiple_of(chunk.at + (1 - d) * size, 256), size)
            if chunk.late:
                cols = chunk.cols
            ref = cot.at[d, blocks[k], :, :, :, cols]
            chunk.core[k] = go(
                remote(ref, ref, chunk.send.at[16 + k], chunk.recv.at[16 + k], core_peer)
            )

        def sum1(chunk, k):
            for h, near, _, half in both_halves(chunk):
                src = (
                    partial.at[blocks[k], :, 1 - x, :, half],
                    partial.at[blocks[k], 1 - y, :, :, half],
                )[h]
                n = 20 + 2 * k + h
                chunk.sum1[k, h] = go(
                    remote(src, chunk.first.at[h, k], chunk.send.at[n], chunk.recv.at[n], near)
                )

        def sum2(chunk, k):
            for h, _, other, half in both_halves(chunk):
                chunk.sum1[k, h].wait_recv()
                row, column, there = ((1 - y, x, 1 - y), (y, 1 - x, 1 - x))[h]
                total = f32(partial[blocks[k], row, column, :, half]) + f32(chunk.first[h, k, there])
                partial[blocks[k], row, column, :, half] = total.astype(bf16)
                n = 28 + 2 * k + h
                chunk.sum2[k, h] = go(
                    remote(
                        partial.at[blocks[k], row, column, :, half], chunk.second.at[h, k],
                        chunk.send.at[n], chunk.recv.at[n], other,
                    )
                )

        def own_total(chunk, k, h):
            mine = f32(partial[blocks[k], y, x, :, chunk.halves[h]])
            return mine + f32(chunk.first[h, k, (y, x)[h]]) + f32(chunk.second[h, k])

        def square_total(chunk, k):
            for h in range(2):
                chunk.sum2[k, h].wait_recv()
                partial[blocks[k], y, x, :, chunk.halves[h]] = own_total(chunk, k, h).astype(bf16)

        def term(chunk, k):
            if chunk.kind == "z":
                return partial.at[blocks[k], y, x, :, chunk.cols]
            return partial.at[blocks[k], :, :, :, chunk.cols]

        def arrived(chunk, slot):
            ref = chunk.along.at[slot]
            remote(ref, ref, chunk.send.at[41], chunk.recv.at[41 + slot], inner_peer).wait_recv()

        def add_term(chunk, k, slots):
            if chunk.kind == "z":
                total = f32(partial[blocks[k], y, x, :, chunk.cols])
                for slot in slots:
                    total = total + f32(chunk.along[slot])
                partial[blocks[k], y, x, :, chunk.cols] = total.astype(bf16)
                return

            wide = 256

            def step(i, _):
                here = pl.ds(pl.multiple_of(i * wide, wide), wide)
                cols = pl.ds(pl.multiple_of(chunk.at + i * wide, wide), wide)
                total = f32(partial[blocks[k], :, :, :, cols])
                for slot in slots:
                    total = total + f32(chunk.along[slot, :, :, :, here])
                partial[blocks[k], :, :, :, cols] = total.astype(bf16)
                return 0

            lax.fori_loop(0, chunk.size // wide, step, 0)

        def sum_z(chunk, k):
            if is_mid:
                arrived(chunk, k)
                add_term(chunk, k, (k,))

            slot = (None, 4 * mid, end, 2 + end)[k]
            to = along(end * inner + mid * outer) if k == 2 else inner_peer
            ref = term(chunk, k)
            go(remote(ref, chunk.along.at[slot], chunk.send.at[41 + k], chunk.recv.at[41 + slot], to))

        def line_total(chunk):
            arrived(chunk, 0)

            if is_mid:
                arrived(chunk, 4)
                add_term(chunk, 0, (0, 4))

            if not is_mid:
                add_term(chunk, 0, (0,))

        def finish_z(chunk):
            arrived(chunk, 0)
            size = chunk.size // 2

            if is_mid:
                arrived(chunk, 4)

            for h in range(2):
                chunk.sum2[0, h].wait_recv()
                here = pl.ds(h * size, size)
                total = own_total(chunk, 0, h) + f32(chunk.along[0, :, here])

                if is_mid:
                    final[:, chunk.halves[h]] = (total + f32(chunk.along[4, :, here])).astype(bf16)

                if not is_mid:
                    final[:, chunk.halves[h]] = total.astype(bf16)

        def finish_x(chunk):
            for h in range(2):
                chunk.sum2[0, h].wait_recv()
                final[:, chunk.halves[h]] = own_total(chunk, 0, h).astype(bf16)

        graded = [0, 0]

        def hidden_step(step, _):
            cols = pl.ds(pl.multiple_of(step * 128, 128), 128)
            g = f32(gate[:, cols])
            u = f32(up[:, cols])
            value = g * jax.nn.sigmoid(g) * u
            hidden[:, cols] = value.astype(bf16)
            hidden_t[d, cols, :] = value.T.astype(bf16)
            return 0

        def forward(chunk, i):
            base = chunk.at + i * STEP
            cols = pl.ds(base, STEP)
            for b in range(ff // BLOCK):
                keep = jnp.concatenate(
                    [
                        jnp.full((16, BLOCK), f32(mask_ref[b, base // BLOCK + c])).astype(bf16)
                        for c in range(STEP // BLOCK)
                    ],
                    axis=1,
                )
                for r in range(BLOCK // 16):
                    rows = pl.ds(b * BLOCK + r * 16, 16)
                    weight[rows, cols] = weight[rows, cols] * keep
            part = jnp.dot(hidden[...], weight[:, cols], preferred_element_type=jnp.float32)
            partial[:, :, :, :, cols] = part.astype(bf16).reshape(partial.shape[:4] + (STEP,))

        def hidden_grad(chunk, part):
            begin, close = graded[part] == 0, graded[part] == len(CHUNKS) - 1
            graded[part] += 1
            wide = 512

            def step(i, _):
                rows = pl.ds(pl.multiple_of(i * wide, wide), wide)
                back = lax.dot_general(
                    cot[d, :, :, :, :, chunk.cols].reshape(tokens, chunk.size),
                    weight[rows, chunk.cols],
                    (((1,), (1,)), ((), ())),
                    preferred_element_type=jnp.float32,
                )
                if not begin:
                    back = back + acc[:, rows]
                if not close:
                    acc[:, rows] = back
                    return 0
                g = f32(gate[:, rows])
                u = f32(up[:, rows])
                s = jax.nn.sigmoid(g)
                gate_grad[:, rows] = (back * u * s * (1.0 + g * (1.0 - s))).astype(bf16)
                up_grad[:, rows] = (back * (g * s)).astype(bf16)
                return 0

            count = ff // wide // 2
            lax.fori_loop(part * count, (part + 1) * count, step, 0)

        def weight_half(chunk):
            size = chunk.size // 2
            base = pl.multiple_of(chunk.at + d * size, 256)
            cols = pl.ds(base, size)
            total = jnp.zeros((ff, size), jnp.float32)
            for core in range(2):
                total = total + jnp.dot(
                    hidden_t[core],
                    cot[core, :, :, :, :, cols].reshape(tokens, size),
                    preferred_element_type=jnp.float32,
                )
            for b in range(ff // BLOCK):
                for c in range(size // BLOCK):
                    keep = f32(mask_ref[b, chunk.at // BLOCK + d * (size // BLOCK) + c]) * scale
                    block = total[b * BLOCK : (b + 1) * BLOCK, c * BLOCK : (c + 1) * BLOCK]
                    at = pl.ds(pl.multiple_of(base + c * BLOCK, BLOCK), BLOCK)
                    weight_grad[pl.ds(b * BLOCK, BLOCK), at] = (block * keep).astype(bf16)
            chunk.half = go(
                remote(
                    weight_grad.at[:, cols], weight_grad.at[:, cols], chunk.send.at[46],
                    chunk.recv.at[46], core_peer,
                )
            )

        def do_loads():
            loads[0].wait()
            loads[1].wait()

        def do_hidden():
            lax.fori_loop(0, ff // 128, hidden_step, 0)
            hidden_core.start()

        def do_forward(c, i):
            if i == 0:
                weight_loads[c].wait()
            forward(chunks[c], i)

        def do_weight(c, _):
            for k in range(4):
                chunks[c].core[k].wait_recv()
            if not chunks[c].late:
                weight_half(chunks[c])

        actions = {
            "loads": do_loads,
            "hidden": do_hidden,
            "own": lambda: loads[2].wait(),
            "hcore": lambda: hidden_core.wait_recv(),
            "fwd": do_forward,
            "wg": do_weight,
            "hg": lambda c, part: hidden_grad(chunks[c], part),
            "gather": lambda c: gather_z(chunks[c]),
            "pass": lambda c, k: pass_z(chunks[c], k),
            "hop1": lambda c, k: hop1(chunks[c], k),
            "hop2": lambda c, k: hop2(chunks[c], k),
            "square": lambda c, k: square(chunks[c], k),
            "core": lambda c, k: to_core(chunks[c], k),
            "sum1": lambda c, k: sum1(chunks[c], k),
            "sum2": lambda c, k: sum2(chunks[c], k),
            "total": lambda c, k: square_total(chunks[c], k),
            "sumz": lambda c, k: sum_z(chunks[c], k),
            "line": lambda c: line_total(chunks[c]),
            "endz": lambda c: finish_z(chunks[c]),
            "endx": lambda c: finish_x(chunks[c]),
        }
        for name, *args in plan:
            actions[name](*args)

        for chunk in chunks:
            if not chunk.late:
                chunk.half.wait_recv()
        for copy in sent:
            copy.wait_send()

        hidden_core.wait_send()

    @pl.when(mid == 1)
    def _():
        run(True, MID_PLAN)

    @pl.when(end == 1)
    def _():
        run(False, END_PLAN)


def keep_in_hbm(array):
    return pltpu.with_memory_space_constraint(array, pltpu.HBM)


def chunk_scratch(rows, width):
    dma = pltpu.SemaphoreType.DMA
    bf16 = jnp.bfloat16
    scratch = []
    for (kind, _), (_, size) in zip(CHUNKS, chunk_columns(width)):
        levels = 4 if kind == "z" else 1
        held = (rows,) if kind == "z" else (2, 2, rows)
        scratch += [
            pltpu.VMEM((2, levels, 2, rows, size // 2), bf16),
            pltpu.VMEM((2, levels, rows, size // 2), bf16),
            pltpu.VMEM((5,) + held + (size,), bf16),
            dma((47,)),
            dma((47,)),
        ]
    return scratch


def fused(gate_pre, up_pre, down_weight, block_mask, out_grad):
    tokens, ff = gate_pre.shape
    rows, width = out_grad.shape
    scale = 1.0 / math.sqrt(tokens * 2)
    hbm = pl.BlockSpec(memory_space=pl.ANY)
    bf16 = jnp.bfloat16
    dma = pltpu.SemaphoreType.DMA
    results = pl.pallas_call(
        functools.partial(fused_kernel, scale),
        out_shape=(
            pltpu.VMEM((rows, width), bf16),
            pltpu.VMEM((tokens, ff), bf16),
            pltpu.VMEM((tokens, ff), bf16),
            pltpu.VMEM((ff, width), bf16),
            pltpu.VMEM((2, 4, 2, 2, rows, width), bf16),
            pltpu.VMEM((2, ff, tokens), bf16),
        ),
        in_specs=[hbm, hbm, hbm, pl.BlockSpec(memory_space=pltpu.SMEM), hbm],
        out_specs=(pl.BlockSpec(memory_space=pltpu.VMEM),) * 6,
        scratch_shapes=[
            pltpu.VMEM((tokens, ff), bf16),
            pltpu.VMEM((tokens, ff), bf16),
            pltpu.VMEM((ff, width), bf16),
            pltpu.VMEM((tokens, ff), bf16),
            pltpu.VMEM((4, 2, 2, rows, width), bf16),
            pltpu.VMEM((tokens, ff), jnp.float32),
            dma((3,)),
            dma((len(CHUNKS),)),
            dma((1,)),
            dma((1,)),
        ]
        + chunk_scratch(rows, width),
        compiler_params=pltpu.CompilerParams(
            collective_id=0, has_side_effects=True, vmem_limit_bytes=38 * 2**20
        ),
        cost_estimate=pl.CostEstimate(
            flops=8 * tokens * ff * width, bytes_accessed=40 * 2**20, transcendentals=2 * tokens * ff
        ),
    )(*(keep_in_hbm(a) for a in (gate_pre, up_pre, down_weight, block_mask, out_grad)))
    return hand_on(scale, block_mask, *results)


def hand_on_kernel(
    scale, mask_hbm, final, gate_grad, up_grad, weight_grad, cot, hidden_t,
    final_hbm, gate_grad_hbm, up_grad_hbm, weight_grad_hbm, mask_ref, tile, store_sem, mask_sem,
):
    ff, width = weight_grad.shape
    tokens = hidden_t.shape[2]
    spans = chunk_columns(width)
    stores = []

    def store(src, dst):
        copy = pltpu.make_async_copy(src, dst, store_sem.at[len(stores)])
        copy.start()
        stores.append(copy)

    mask_load = pltpu.make_async_copy(mask_hbm, mask_ref, mask_sem.at[0])
    mask_load.start()
    runs = []
    for c, (at, size) in enumerate(spans):
        if c in LATE:
            continue
        if runs and sum(runs[-1]) == at:
            at, size = runs[-1][0], runs[-1][1] + size
            runs.pop()
        runs.append((at, size))
    for at, size in runs:
        store(weight_grad.at[:, pl.ds(at, size)], weight_grad_hbm.at[:, pl.ds(at, size)])
    store(gate_grad, gate_grad_hbm)
    store(up_grad, up_grad_hbm)
    store(final, final_hbm)
    wide = 512
    put = 0
    mask_load.wait()
    for c in LATE:
        at, size = spans[c]
        for first in range(at, at + size, wide):
            cols = pl.ds(first, wide)
            total = jnp.zeros((ff, wide), jnp.float32)
            for core in range(2):
                total = total + jnp.dot(
                    hidden_t[core],
                    cot[core, :, :, :, :, cols].reshape(tokens, wide),
                    preferred_element_type=jnp.float32,
                )
            for b in range(ff // BLOCK):
                for n in range(wide // BLOCK):
                    keep = f32(mask_ref[b, first // BLOCK + n]) * scale
                    block = total[b * BLOCK : (b + 1) * BLOCK, n * BLOCK : (n + 1) * BLOCK]
                    tile[pl.ds(b * BLOCK, BLOCK), pl.ds(put + n * BLOCK, BLOCK)] = (
                        block * keep
                    ).astype(jnp.bfloat16)
            store(tile.at[:, pl.ds(put, wide)], weight_grad_hbm.at[:, cols])
            put += wide
    for copy in stores:
        copy.wait()


def hand_on(scale, block_mask, *arrays):
    ff, width = arrays[3].shape
    late = sum(chunk_columns(width)[c][1] for c in LATE)
    held = pl.BlockSpec(memory_space=pltpu.VMEM)
    return pl.pallas_call(
        functools.partial(hand_on_kernel, scale),
        out_shape=tuple(jax.ShapeDtypeStruct(a.shape, a.dtype) for a in arrays[:4]),
        in_specs=[pl.BlockSpec(memory_space=pl.ANY)] + [held] * len(arrays),
        out_specs=(pl.BlockSpec(memory_space=pl.ANY),) * 4,
        scratch_shapes=[
            pltpu.SMEM(block_mask.shape, jnp.int32),
            pltpu.VMEM((ff, late), jnp.bfloat16),
            pltpu.SemaphoreType.DMA((len(CHUNKS) + 3 + late // 512,)),
            pltpu.SemaphoreType.DMA((1,)),
        ],
        compiler_params=pltpu.CompilerParams(vmem_limit_bytes=12 * 2**20),
    )(keep_in_hbm(block_mask), *(pltpu.with_memory_space_constraint(a, pltpu.VMEM) for a in arrays))


def local(gate_pre, up_pre, down_weight, block_mask, out_grad):
    blk_rows, blk_cols = block_mask.shape
    ff_local, width = down_weight.shape
    masked = (
        down_weight.reshape(blk_rows, 128, blk_cols, 128)
        * block_mask.astype(jnp.bfloat16)[:, None, :, None]
    ).reshape(ff_local, width)
    gate_val = gate_pre.astype(jnp.float32)
    up_val = up_pre.astype(jnp.float32)
    sigmoid_gate = jax.nn.sigmoid(gate_val)
    silu_gate = gate_val * sigmoid_gate
    hidden = (silu_gate * up_val).astype(jnp.bfloat16)
    layer_out = lax.psum_scatter(
        jnp.dot(hidden, masked, preferred_element_type=jnp.float32),
        "tensor",
        scatter_dimension=0,
        tiled=True,
    ).astype(jnp.bfloat16)
    cot_rows = lax.all_gather(out_grad, "tensor", axis=0, tiled=True)
    hidden_grad = lax.dot_general(
        cot_rows, masked, (((1,), (1,)), ((), ())), preferred_element_type=jnp.float32
    )
    gate_grad = (
        hidden_grad * up_val * sigmoid_gate * (1.0 + gate_val * (1.0 - sigmoid_gate))
    ).astype(jnp.bfloat16)
    up_grad = (hidden_grad * silu_gate).astype(jnp.bfloat16)
    tokens_all = out_grad.shape[0] * lax.axis_size("tensor") * lax.axis_size("dp")
    grad_scale = 1.0 / math.sqrt(tokens_all)
    partial_grad = (
        lax.dot_general(
            hidden, cot_rows, (((0,), (0,)), ((), ())), preferred_element_type=jnp.float32
        )
        * grad_scale
    )
    blocked = (
        partial_grad.reshape(blk_rows, 128, blk_cols, 128)
        * block_mask.astype(jnp.float32)[:, None, :, None]
    )
    summed = lax.psum(blocked.reshape(ff_local, width), "dp")
    weight_grad = summed.astype(jnp.bfloat16)
    return (layer_out, gate_grad, up_grad, weight_grad)


def solution(mesh):
    grouped = mesh.shape["dp"] == 2 and mesh.shape["tensor"] == 16
    return jax.shard_map(
        fused if grouped else local,
        mesh=mesh,
        in_specs=(
            P("dp", "tensor"),
            P("dp", "tensor"),
            P("tensor", None),
            P("tensor", None),
            P(("dp", "tensor"), None),
        ),
        out_specs=(
            P(("dp", "tensor"), None),
            P("dp", "tensor"),
            P("dp", "tensor"),
            P("tensor", None),
        ),
        check_vma=False,
    )
```
